32 devices in a mesh: dp: 8 (over z, core), fsdp: 4 (over y, x).
Axes of the slice: x: 2, y: 2, z: 4, core: 2. Of those that a mesh axis runs over, the one named last changes fastest.
Arguments:
- activations: bfloat16 [6144, 4096], P(('dp', 'fsdp')), may hold values from -12 to 12
- cotangent: bfloat16 [6144, 512], P(('dp', 'fsdp')), may hold values from -6 to 6
- weight: bfloat16 [4096, 512], P('fsdp'), may hold values from -0.09375 to 0.09375
- momentum: float32 [8, 4096, 512], P('dp', 'fsdp'), may hold values from -256 to 256
- positions: int32 [16, 32, 512], P('fsdp'), may hold values from 0 to 255, as said below
Outputs:
- grad_input: bfloat16 [6144, 4096], P(('dp', 'fsdp'))
- new_momentum: float32 [8, 4096, 512], P('dp', 'fsdp')
- update: bfloat16 [4096, 512], P('fsdp')
The draws below stay inside these ranges and needn't reach their ends.
Inputs may be any that keep to these rules, and one draw needn't show every extreme that they name: For each block b and column c the 32 values positions[b, :, c] are distinct.
All inputs are finite; a program needn't handle non-finite values.
Results may differ from the reference program's by a relative error of at most 0.023.
Values may be sent and summed in bfloat16 or wider, within the bound.
No kernel may reach another device: no remote copies, remote signals or barrier semaphores. Data moves between devices by JAX's collectives and lax.ppermute only.
A program may use at most 64 MiB of HBM per device.

```python
import jax
import jax.numpy as jnp
from jax import lax

D_WIN = 4096
KV = 512
SPAN = 256
TOPK = 32
TOK_DEV = 192
TOKENS = 6144
N_DP = 8
N_FSDP = 4


def draw_positions(key, part):
    shape = (D_WIN // SPAN, SPAN, KV)
    scores = jax.random.randint(key, shape, 0, 1 << 20, dtype=jnp.int32)
    ranked = scores * SPAN + lax.broadcasted_iota(jnp.int32, shape, 1)
    order = jnp.argsort(ranked, axis=1, stable=True)
    return order[:, :TOPK, :].astype(jnp.int32)


def strengthened(values, stream_key, source, target, shards_of, factor):
    def block_of(axis_at):
        return (jnp.arange(values.shape[axis_at]) // (values.shape[axis_at] // shards_of)).reshape((-1,) + (1,) * (values.ndim - 1 - axis_at))

    one_side = jax.random.permutation(stream_key, shards_of)[block_of(target)]
    second = (block_of(target) + shards_of // 2) % shards_of
    return jnp.where((block_of(source) == one_side) | (block_of(source) == second), factor * values, values)


def steps_of(rng, shape, shards, least, largest):
    level, own = 1.0, jax.random.fold_in(rng, 6)
    for axis_at, blocks in shards:
        draws = jnp.exp(jax.random.uniform(jax.random.fold_in(own, axis_at), (blocks,), jnp.float32, least / len(shards), largest / len(shards)))
        level = level * jnp.repeat(draws, shape[axis_at] // blocks).reshape([-1 if axis == axis_at else 1 for axis in range(len(shape))])
    return level


def centred(own_key, dims, deviation, reach, cuts=(), kind=jnp.bfloat16):
    factor_of = steps_of(own_key, dims, cuts, -0.22, 0.18) if cuts else 1.0
    array = jax.random.normal(own_key, dims, jnp.float32) * deviation * factor_of
    return jnp.minimum(jnp.maximum(array, -reach), reach).astype(kind)


def bell_draw_with(rng, shape, scale, bound, cuts, heavy, kind=jnp.bfloat16):
    result = scale * jax.random.normal(rng, shape, jnp.float32)
    if cuts:
        result = result * steps_of(rng, shape, cuts, -0.22, 0.18)
    return jnp.clip(strengthened(result, jax.random.fold_in(rng, 3), *heavy), -bound, bound).astype(kind)


def setup_inputs(seed: int = 0) -> dict:
    splits = jax.random.split(jax.random.key(seed), 6)
    return {
        "activations": bell_draw_with(splits[0], (TOKENS, D_WIN), 1.0, 12.0, ((0, 32),), (0, 1, 32, 2.75)),
        "cotangent": centred(splits[1], (TOKENS, KV), 1.0, 6.0, ((0, 32),)),
        "weight": centred(splits[2], (D_WIN, KV), D_WIN ** -0.5, 0.09375, ((0, 4),)),
        "momentum": centred(splits[3], (N_DP, D_WIN, KV), 40.0, 256.0, ((0, 8), (1, 4)), jnp.float32),
        "positions": draw_positions(jax.random.fold_in(splits[5], 71), 0),
    }


def transform_table(length):
    freq = jnp.arange(length, dtype=jnp.float32)[:, None]
    place = jnp.arange(length, dtype=jnp.float32)[None, :]
    angles = jnp.pi * (2.0 * place + 1.0) * freq / (2.0 * length)
    scales = jnp.where(freq == 0.0, jnp.sqrt(1.0 / length), jnp.sqrt(2.0 / length))
    return scales * jnp.cos(angles)

def forward_blocks(table, blocks):
    return jnp.einsum('kn,bnc->bkc', table, blocks, precision=lax.Precision.HIGHEST)

def inverse_blocks(table, coeffs):
    return jnp.einsum('kn,bkc->bnc', table, coeffs, precision=lax.Precision.HIGHEST)

def spread_band(values, positions, length):
    blocks, picks, columns = values.shape
    block_index = jnp.arange(blocks, dtype=jnp.int32)[:, None, None]
    column_index = jnp.arange(columns, dtype=jnp.int32)[None, None, :]
    dense = jnp.zeros((blocks, length, columns), values.dtype)
    return dense.at[block_index, positions, column_index].add(values)

def reference(activations, cotangent, weight, momentum, positions):
    table = transform_table(SPAN)
    inputs = activations.reshape(N_DP, N_FSDP, TOK_DEV, D_WIN)
    grads = cotangent.reshape(N_DP, N_FSDP, TOK_DEV, KV)

    def one_replica(packed):
        replica_inputs, replica_grads, replica_moment = packed
        flat_grads = replica_grads.reshape(N_FSDP * TOK_DEV, KV)
        grad_input = jnp.dot(flat_grads, weight.T, preferred_element_type=jnp.float32).astype(jnp.bfloat16)
        partials = jnp.einsum('stf,stj->sfj', replica_inputs.astype(jnp.float32), replica_grads.astype(jnp.float32))
        partials = partials.astype(jnp.bfloat16).astype(jnp.float32)
        gradient = lax.optimization_barrier(jnp.sum(partials, axis=0))
        moment = 0.999 * replica_moment + gradient
        blocks = moment.reshape(D_WIN // SPAN, SPAN, KV)
        coeffs = forward_blocks(table, blocks)
        picked = jnp.take_along_axis(coeffs, positions, axis=1)
        kept = blocks - inverse_blocks(table, spread_band(picked, positions, SPAN))
        return (grad_input, kept.reshape(D_WIN, KV), picked.astype(jnp.bfloat16))
    grad_input, new_momentum, bands = lax.map(one_replica, (inputs, grads, momentum))
    mean_band = lax.optimization_barrier(jnp.sum(bands.astype(jnp.float32), axis=0)) / N_DP
    update = inverse_blocks(table, spread_band(mean_band, positions, SPAN)).reshape(D_WIN, KV).astype(jnp.bfloat16)
    return (grad_input.reshape(N_DP * N_FSDP * TOK_DEV, D_WIN), new_momentum, update)
```

```python
import functools

import jax
import jax.numpy as jnp
import numpy as np
from jax import lax
from jax.experimental import pallas as pl
from jax.experimental.pallas import tpu as pltpu
from jax.sharding import PartitionSpec as P

SPAN = 256
MOMENTUM_DECAY = 0.999
LANES = 128
SUBLANES = 8
VMEM_LIMIT = 48 * 1024 * 1024


def transform_table():
    freq = np.arange(SPAN, dtype=np.float64)[:, None]
    place = np.arange(SPAN, dtype=np.float64)[None, :]
    scales = np.where(freq == 0.0, np.sqrt(1.0 / SPAN), np.sqrt(2.0 / SPAN))
    table = scales * np.cos(np.pi * (2.0 * place + 1.0) * freq / (2.0 * SPAN))
    high = table.astype(jnp.bfloat16)
    low = (table - high.astype(np.float64)).astype(jnp.bfloat16)
    return high, low


def two_terms(x):
    high = x.astype(jnp.bfloat16)
    return high, (x - high.astype(jnp.float32)).astype(jnp.bfloat16)


def dot(left, right):
    return jnp.dot(left, right, preferred_element_type=jnp.float32)


def split_dot(table_high, table_low, x):
    high, low = two_terms(x)
    return dot(table_high, high) + (dot(table_high, low) + dot(table_low, high))


def params(**more):
    return pltpu.CompilerParams(vmem_limit_bytes=VMEM_LIMIT, **more)


def inverse_index_kernel(positions_ref, inverse_ref):
    picks, columns = positions_ref.shape[1:]
    chunk = 64

    def one_chunk(at, carry):
        start = pl.multiple_of(at * chunk, chunk)
        for c in range(0, columns, LANES):
            where = positions_ref[0, :, c : c + LANES]
            level = lax.broadcasted_iota(jnp.int32, (chunk, LANES), 0) + start
            found = jnp.full((chunk, LANES), -1, jnp.int32)
            for i in range(picks):
                found = jnp.where(where[i : i + 1, :] == level, i, found)
            inverse_ref[0, pl.ds(start, chunk), c : c + LANES] = found
        return carry

    lax.fori_loop(0, SPAN // chunk, one_chunk, 0)


def inverse_index(positions):
    blocks, picks, columns = positions.shape
    return pl.pallas_call(
        inverse_index_kernel,
        out_shape=jax.ShapeDtypeStruct((blocks, SPAN, columns), jnp.int32),
        grid=(blocks,),
        in_specs=[pl.BlockSpec((1, picks, columns), lambda b: (b, 0, 0))],
        out_specs=pl.BlockSpec((1, SPAN, columns), lambda b: (b, 0, 0)),
        compiler_params=params(),
        cost_estimate=pl.CostEstimate(
            flops=2 * blocks * picks * SPAN * columns,
            bytes_accessed=4 * blocks * SPAN * columns,
            transcendentals=0,
        ),
        name="inverse_index",
    )(positions)


def outer_kernel(groups, *refs):
    weight_ref = refs[groups]
    for s in range(groups):
        refs[groups + 1 + s][...] = lax.dot_general(
            refs[s][...],
            weight_ref[...],
            (((1,), (1,)), ((), ())),
            preferred_element_type=jnp.float32,
        ).astype(jnp.bfloat16)


def input_gradients(cotangents, weight):
    tokens, outputs = cotangents[0].shape
    rows = weight.shape[0]
    groups = len(cotangents)
    return pl.pallas_call(
        functools.partial(outer_kernel, groups),
        out_shape=[jax.ShapeDtypeStruct((tokens, rows), jnp.bfloat16)] * groups,
        compiler_params=params(),
        cost_estimate=pl.CostEstimate(
            flops=2 * groups * tokens * rows * outputs,
            bytes_accessed=2 * (groups * tokens * (rows + outputs) + rows * outputs),
            transcendentals=0,
        ),
        name="input_gradients",
    )(*cotangents, weight)


def moment_kernel(groups, place_ref, *refs):
    inputs, cotangents = refs[:groups], refs[groups : 2 * groups]
    momentum_ref, positions_ref, inverse_ref, high_ref, low_ref = refs[2 * groups : 2 * groups + 5]
    moment_ref, masked_ref, mine_ref, theirs_ref, coeffs_ref = refs[2 * groups + 5 :]
    picks, columns = positions_ref.shape[1:]
    gradient = None
    for s in range(groups):
        term = lax.dot_general(
            inputs[s][...],
            cotangents[s][...],
            (((0,), (0,)), ((), ())),
            preferred_element_type=jnp.float32,
        )
        gradient = term if gradient is None else gradient + term
    moment = MOMENTUM_DECAY * momentum_ref[0] + gradient
    moment_ref[...] = moment
    coeffs = split_dot(high_ref[...], low_ref[...], moment)
    coeffs_ref[...] = coeffs
    masked_ref[...] = jnp.where(inverse_ref[0] >= 0, coeffs, 0.0).astype(jnp.bfloat16)
    half = picks // 2
    parts = []
    for c in range(0, columns, LANES):
        found = []
        for p in range(0, picks, SUBLANES):
            where = positions_ref[0, p : p + SUBLANES, c : c + LANES]
            inside, group = where & (SUBLANES - 1), where // SUBLANES
            total = jnp.zeros((SUBLANES, LANES), jnp.float32)
            for g in range(SPAN // SUBLANES):
                rows = coeffs_ref[g * SUBLANES : (g + 1) * SUBLANES, c : c + LANES]
                total = jnp.where(
                    group == g, jnp.take_along_axis(rows, inside, axis=0), total
                )
            found.append(total)
        parts.append(jnp.concatenate(found, axis=0).astype(jnp.bfloat16))
    bands = jnp.concatenate(parts, axis=1)
    second = place_ref[1] == 1
    mine_ref[0] = jnp.where(second, bands[half:], bands[:half])
    theirs_ref[0] = jnp.where(second, bands[:half], bands[half:])


def moments(place, own_inputs, inputs, cotangents, momentum, positions, inverse, high, low):
    groups = len(cotangents)
    tokens, columns = cotangents[0].shape
    blocks, picks, _ = positions.shape
    whole = lambda b, place: (0, 0)
    half_shape = jax.ShapeDtypeStruct((blocks, picks // 2, columns), jnp.bfloat16)
    by_block = lambda b, place: (b, 0, 0)
    return pl.pallas_call(
        functools.partial(moment_kernel, groups),
        out_shape=[
            jax.ShapeDtypeStruct((blocks * SPAN, columns), jnp.float32),
            jax.ShapeDtypeStruct((blocks * SPAN, columns), jnp.bfloat16),
            half_shape,
            half_shape,
        ],
        grid_spec=pltpu.PrefetchScalarGridSpec(
            num_scalar_prefetch=1,
            grid=(blocks,),
            in_specs=[pl.BlockSpec((tokens, SPAN), lambda b, place: (0, place[0] * blocks + b))]
            + [pl.BlockSpec((tokens, SPAN), lambda b, place: (0, b))] * (groups - 1)
            + [pl.BlockSpec((tokens, columns), whole)] * groups
            + [
                pl.BlockSpec((1, SPAN, columns), lambda b, place: (0, b, 0)),
                pl.BlockSpec((1, picks, columns), by_block),
                pl.BlockSpec((1, SPAN, columns), by_block),
                pl.BlockSpec((SPAN, SPAN), whole),
                pl.BlockSpec((SPAN, SPAN), whole),
            ],
            out_specs=[
                pl.BlockSpec((SPAN, columns), lambda b, place: (b, 0)),
                pl.BlockSpec((SPAN, columns), lambda b, place: (b, 0)),
                pl.BlockSpec((1, picks // 2, columns), by_block),
                pl.BlockSpec((1, picks // 2, columns), by_block),
            ],
            scratch_shapes=[pltpu.VMEM((SPAN, columns), jnp.float32)],
        ),
        compiler_params=params(),
        cost_estimate=pl.CostEstimate(
            flops=2 * blocks * SPAN * columns * (groups * tokens + 3 * SPAN),
            bytes_accessed=blocks * SPAN * (groups * tokens * 2 + 14 * columns),
            transcendentals=0,
        ),
        name="moment",
    )(place, own_inputs, *inputs, *cotangents, momentum, positions, inverse, high, low)


def feedback_kernel(moment_ref, masked_ref, high_ref, low_ref, kept_ref):
    sent = dot(high_ref[...], masked_ref[...]) + dot(low_ref[...], masked_ref[...])
    kept_ref[0] = moment_ref[...] - sent


def feedback(moment, masked, high, low):
    rows, columns = moment.shape
    whole = lambda b: (0, 0)
    return pl.pallas_call(
        feedback_kernel,
        out_shape=jax.ShapeDtypeStruct((1, rows, columns), jnp.float32),
        grid=(rows // SPAN,),
        in_specs=[
            pl.BlockSpec((SPAN, columns), lambda b: (b, 0)),
            pl.BlockSpec((SPAN, columns), lambda b: (b, 0)),
            pl.BlockSpec((SPAN, SPAN), whole),
            pl.BlockSpec((SPAN, SPAN), whole),
        ],
        out_specs=pl.BlockSpec((1, SPAN, columns), lambda b: (0, b, 0)),
        compiler_params=params(),
        cost_estimate=pl.CostEstimate(
            flops=4 * rows * columns * SPAN, bytes_accessed=10 * rows * columns, transcendentals=0
        ),
        name="feedback",
    )(moment, masked, high, low)


def decode_kernel(replicas, place_ref, mine_ref, theirs_ref, inverse_ref, high_ref, low_ref, update_ref, dense_ref):
    columns = mine_ref.shape[2]
    half = mine_ref.shape[1]
    second = place_ref[1] == 1
    mine = mine_ref[0].astype(jnp.float32) * (1.0 / replicas)
    theirs = theirs_ref[0].astype(jnp.float32) * (1.0 / replicas)
    first_half = jnp.where(second, theirs, mine)
    second_half = jnp.where(second, mine, theirs)
    for c in range(0, columns, LANES):
        source = [
            part[p : p + SUBLANES, c : c + LANES]
            for part in (first_half, second_half)
            for p in range(0, half, SUBLANES)
        ]
        for g in range(0, SPAN, SUBLANES):
            pick = inverse_ref[0, g : g + SUBLANES, c : c + LANES]
            inside, group = pick & (SUBLANES - 1), pick >> 3
            total = jnp.zeros((SUBLANES, LANES), jnp.float32)
            for s, rows in enumerate(source):
                total = jnp.where(group == s, jnp.take_along_axis(rows, inside, axis=0), total)
            dense_ref[g : g + SUBLANES, c : c + LANES] = total
    update_ref[...] = split_dot(high_ref[...], low_ref[...], dense_ref[...]).astype(jnp.bfloat16)


def decode(place, mine, theirs, inverse, high, low, replicas):
    blocks, half, columns = mine.shape
    whole = lambda b, place: (0, 0)
    by_block = lambda b, place: (b, 0, 0)
    return pl.pallas_call(
        functools.partial(decode_kernel, replicas),
        out_shape=jax.ShapeDtypeStruct((blocks * SPAN, columns), jnp.bfloat16),
        grid_spec=pltpu.PrefetchScalarGridSpec(
            num_scalar_prefetch=1,
            grid=(blocks,),
            in_specs=[
                pl.BlockSpec((1, half, columns), by_block),
                pl.BlockSpec((1, half, columns), by_block),
                pl.BlockSpec((1, SPAN, columns), by_block),
                pl.BlockSpec((SPAN, SPAN), whole),
                pl.BlockSpec((SPAN, SPAN), whole),
            ],
            out_specs=pl.BlockSpec((SPAN, columns), lambda b, place: (b, 0)),
            scratch_shapes=[pltpu.VMEM((SPAN, columns), jnp.float32)],
        ),
        compiler_params=params(),
        cost_estimate=pl.CostEstimate(
            flops=6 * blocks * SPAN * SPAN * columns,
            bytes_accessed=6 * blocks * SPAN * columns,
            transcendentals=0,
        ),
        name="decode",
    )(place, mine, theirs, inverse, high, low)


def assemble_kernel(groups, place_ref, *refs):
    parts, out_ref, sems = refs[:groups], refs[groups], refs[groups + 1]
    width = parts[0].shape[1]
    copies = []
    for m in range(groups):
        at = pl.multiple_of((place_ref[0] ^ m) * width, width)
        copies.append(pltpu.make_async_copy(parts[m], out_ref.at[:, pl.ds(at, width)], sems.at[m]))
    for copy in copies:
        copy.start()
    for copy in copies:
        copy.wait()


def assemble(place, parts):
    groups = len(parts)
    tokens, width = parts[0].shape
    return pl.pallas_call(
        functools.partial(assemble_kernel, groups),
        out_shape=jax.ShapeDtypeStruct((tokens, groups * width), jnp.bfloat16),
        in_specs=[pl.BlockSpec(memory_space=pltpu.SMEM)] + [pl.BlockSpec(memory_space=pl.ANY)] * groups,
        out_specs=pl.BlockSpec(memory_space=pl.ANY),
        scratch_shapes=[pltpu.SemaphoreType.DMA((groups,))],
        compiler_params=params(),
        cost_estimate=pl.CostEstimate(
            flops=0, bytes_accessed=4 * groups * tokens * width, transcendentals=0
        ),
        name="assemble",
    )(place, *parts)


def swap(x, axis, mask):
    size = lax.axis_size(axis)
    return lax.ppermute(x, axis, [(s, s ^ mask) for s in range(size)])


def sum_over_chips(x):
    replicas = lax.axis_size("dp")
    stride = 2
    total = x
    while stride < replicas:
        sent = total.astype(jnp.bfloat16)
        parts = [sent] + [swap(sent, "dp", stride * m) for m in (1, 2, 3) if stride * m < replicas]
        parts = [part.astype(jnp.float32) for part in parts]
        total = parts[0] + parts[1] if len(parts) == 2 else (parts[0] + parts[1]) + (parts[2] + parts[3])
        stride *= 4
    return total.astype(jnp.bfloat16)


def on_device(activations, cotangent, weight, momentum, positions):
    groups, replicas = lax.axis_size("fsdp"), lax.axis_size("dp")
    rows = weight.shape[0]
    index = lax.axis_index("fsdp")
    place = jnp.stack([index, lax.axis_index("dp") % 2]).astype(jnp.int32)
    high, low = transform_table()

    cotangents = [cotangent] + [swap(cotangent, "fsdp", m) for m in range(1, groups)]
    inputs = [
        swap(lax.dynamic_slice_in_dim(activations, (index ^ m) * rows, rows, 1), "fsdp", m)
        for m in range(1, groups)
    ]
    inverse = inverse_index(positions)
    outer = input_gradients(cotangents, weight)
    grad_input = assemble(
        place, [outer[0]] + [swap(outer[m], "fsdp", m) for m in range(1, groups)]
    )

    moment, masked, mine, theirs = moments(
        place, activations, inputs, cotangents, momentum, positions, inverse, high, low
    )
    chip = mine.astype(jnp.float32) + swap(theirs, "dp", 1).astype(jnp.float32)
    new_momentum = feedback(moment, masked, high.T, low.T)
    summed = sum_over_chips(chip)
    update = decode(place, summed, swap(summed, "dp", 1), inverse, high.T, low.T, replicas)
    return grad_input, new_momentum, update


def solution(mesh):
    placed = (
        P(("dp", "fsdp"), None),
        P(("dp", "fsdp"), None),
        P("fsdp", None),
        P("dp", "fsdp", None),
        P("fsdp", None, None),
    )
    return jax.shard_map(
        on_device,
        mesh=mesh,
        in_specs=placed,
        out_specs=(P(("dp", "fsdp"), None), P("dp", "fsdp", None), P("fsdp", None)),
        check_vma=False,
    )
```

```python
import functools

import jax
import jax.numpy as jnp
import numpy as np
from jax import lax
from jax.experimental import pallas as pl
from jax.experimental.pallas import tpu as pltpu
from jax.sharding import PartitionSpec as P

SPAN = 256
MOMENTUM_DECAY = 0.999
LANES = 128
SUBLANES = 8
VMEM_LIMIT = 16 * 1024 * 1024


def transform_table():
    freq = np.arange(SPAN, dtype=np.float64)[:, None]
    place = np.arange(SPAN, dtype=np.float64)[None, :]
    scales = np.where(freq == 0.0, np.sqrt(1.0 / SPAN), np.sqrt(2.0 / SPAN))
    table = scales * np.cos(np.pi * (2.0 * place + 1.0) * freq / (2.0 * SPAN))
    high = table.astype(jnp.bfloat16)
    low = (table - high.astype(np.float64)).astype(jnp.bfloat16)
    return high, low


def two_terms(x):
    high = x.astype(jnp.bfloat16)
    return high, (x - high.astype(jnp.float32)).astype(jnp.bfloat16)


def dot(left, right):
    return jnp.dot(left, right, preferred_element_type=jnp.float32)


def split_dot(table_high, table_low, x):
    high, low = two_terms(x)
    return dot(table_high, high) + (dot(table_high, low) + dot(table_low, high))


def params(**more):
    return pltpu.CompilerParams(vmem_limit_bytes=VMEM_LIMIT, **more)


def inverse_index_kernel(positions_ref, inverse_ref):
    picks, columns = positions_ref.shape[1:]
    chunk = 64

    def one_chunk(at, carry):
        start = pl.multiple_of(at * chunk, chunk)
        for c in range(0, columns, LANES):
            where = positions_ref[0, :, c : c + LANES]
            level = lax.broadcasted_iota(jnp.int32, (chunk, LANES), 0) + start
            found = jnp.full((chunk, LANES), -1, jnp.int32)
            for i in range(picks):
                found = jnp.where(where[i : i + 1, :] == level, i, found)
            inverse_ref[0, pl.ds(start, chunk), c : c + LANES] = found
        return carry

    lax.fori_loop(0, SPAN // chunk, one_chunk, 0)


def inverse_index(positions):
    blocks, picks, columns = positions.shape
    return pl.pallas_call(
        inverse_index_kernel,
        out_shape=jax.ShapeDtypeStruct((blocks, SPAN, columns), jnp.int32),
        grid=(blocks,),
        in_specs=[pl.BlockSpec((1, picks, columns), lambda b: (b, 0, 0))],
        out_specs=pl.BlockSpec((1, SPAN, columns), lambda b: (b, 0, 0)),
        compiler_params=params(),
        cost_estimate=pl.CostEstimate(
            flops=2 * blocks * picks * SPAN * columns,
            bytes_accessed=4 * blocks * SPAN * columns,
            transcendentals=0,
        ),
        name="inverse_index",
    )(positions)


def outer_kernel(groups, *refs):
    weight_ref = refs[groups]
    for s in range(groups):
        refs[groups + 1 + s][...] = lax.dot_general(
            refs[s][...],
            weight_ref[...],
            (((1,), (1,)), ((), ())),
            preferred_element_type=jnp.float32,
        ).astype(jnp.bfloat16)


def input_gradients(cotangents, weight):
    tokens, outputs = cotangents[0].shape
    rows = weight.shape[0]
    groups = len(cotangents)
    return pl.pallas_call(
        functools.partial(outer_kernel, groups),
        out_shape=[jax.ShapeDtypeStruct((tokens, rows), jnp.bfloat16)] * groups,
        compiler_params=params(),
        cost_estimate=pl.CostEstimate(
            flops=2 * groups * tokens * rows * outputs,
            bytes_accessed=2 * (groups * tokens * (rows + outputs) + rows * outputs),
            transcendentals=0,
        ),
        name="input_gradients",
    )(*cotangents, weight)


def moment_kernel(groups, place_ref, *refs):
    inputs, cotangents = refs[:groups], refs[groups : 2 * groups]
    momentum_ref, positions_ref, inverse_ref, high_ref, low_ref = refs[2 * groups : 2 * groups + 5]
    moment_ref, masked_ref, mine_ref, theirs_ref, coeffs_ref = refs[2 * groups + 5 :]
    picks, columns = positions_ref.shape[1:]
    gradient = None
    for s in range(groups):
        term = lax.dot_general(
            inputs[s][...],
            cotangents[s][...],
            (((0,), (0,)), ((), ())),
            preferred_element_type=jnp.float32,
        )
        gradient = term if gradient is None else gradient + term
    moment = MOMENTUM_DECAY * momentum_ref[0] + gradient
    moment_ref[...] = moment
    coeffs = split_dot(high_ref[...], low_ref[...], moment)
    coeffs_ref[...] = coeffs
    masked_ref[...] = jnp.where(inverse_ref[0] >= 0, coeffs, 0.0).astype(jnp.bfloat16)
    half = picks // 2
    parts = []
    for c in range(0, columns, LANES):
        found = []
        for p in range(0, picks, SUBLANES):
            where = positions_ref[0, p : p + SUBLANES, c : c + LANES]
            inside, group = where & (SUBLANES - 1), where // SUBLANES
            total = jnp.zeros((SUBLANES, LANES), jnp.float32)
            for g in range(SPAN // SUBLANES):
                rows = coeffs_ref[g * SUBLANES : (g + 1) * SUBLANES, c : c + LANES]
                total = jnp.where(
                    group == g, jnp.take_along_axis(rows, inside, axis=0), total
                )
            found.append(total)
        parts.append(jnp.concatenate(found, axis=0).astype(jnp.bfloat16))
    bands = jnp.concatenate(parts, axis=1)
    second = place_ref[1] == 1
    mine_ref[0] = jnp.where(second, bands[half:], bands[:half])
    theirs_ref[0] = jnp.where(second, bands[:half], bands[half:])


def moments(place, own_inputs, inputs, cotangents, momentum, positions, inverse, high, low):
    groups = len(cotangents)
    tokens, columns = cotangents[0].shape
    blocks, picks, _ = positions.shape
    whole = lambda b, place: (0, 0)
    half_shape = jax.ShapeDtypeStruct((blocks, picks // 2, columns), jnp.bfloat16)
    by_block = lambda b, place: (b, 0, 0)
    return pl.pallas_call(
        functools.partial(moment_kernel, groups),
        out_shape=[
            jax.ShapeDtypeStruct((blocks * SPAN, columns), jnp.float32),
            jax.ShapeDtypeStruct((blocks * SPAN, columns), jnp.bfloat16),
            half_shape,
            half_shape,
        ],
        grid_spec=pltpu.PrefetchScalarGridSpec(
            num_scalar_prefetch=1,
            grid=(blocks,),
            in_specs=[pl.BlockSpec((tokens, SPAN), lambda b, place: (0, place[0] * blocks + b))]
            + [pl.BlockSpec((tokens, SPAN), lambda b, place: (0, b))] * (groups - 1)
            + [pl.BlockSpec((tokens, columns), whole)] * groups
            + [
                pl.BlockSpec((1, SPAN, columns), lambda b, place: (0, b, 0)),
                pl.BlockSpec((1, picks, columns), by_block),
                pl.BlockSpec((1, SPAN, columns), by_block),
                pl.BlockSpec((SPAN, SPAN), whole),
                pl.BlockSpec((SPAN, SPAN), whole),
            ],
            out_specs=[
                pl.BlockSpec((SPAN, columns), lambda b, place: (b, 0)),
                pl.BlockSpec((SPAN, columns), lambda b, place: (b, 0)),
                pl.BlockSpec((1, picks // 2, columns), by_block),
                pl.BlockSpec((1, picks // 2, columns), by_block),
            ],
            scratch_shapes=[pltpu.VMEM((SPAN, columns), jnp.float32)],
        ),
        compiler_params=params(),
        cost_estimate=pl.CostEstimate(
            flops=2 * blocks * SPAN * columns * (groups * tokens + 3 * SPAN),
            bytes_accessed=blocks * SPAN * (groups * tokens * 2 + 14 * columns),
            transcendentals=0,
        ),
        name="moment",
    )(place, own_inputs, *inputs, *cotangents, momentum, positions, inverse, high, low)


def feedback_kernel(moment_ref, masked_ref, high_ref, low_ref, kept_ref):
    sent = dot(high_ref[...], masked_ref[...]) + dot(low_ref[...], masked_ref[...])
    kept_ref[0] = moment_ref[...] - sent


def feedback(moment, masked, high, low):
    rows, columns = moment.shape
    whole = lambda b: (0, 0)
    return pl.pallas_call(
        feedback_kernel,
        out_shape=jax.ShapeDtypeStruct((1, rows, columns), jnp.float32),
        grid=(rows // SPAN,),
        in_specs=[
            pl.BlockSpec((SPAN, columns), lambda b: (b, 0)),
            pl.BlockSpec((SPAN, columns), lambda b: (b, 0)),
            pl.BlockSpec((SPAN, SPAN), whole),
            pl.BlockSpec((SPAN, SPAN), whole),
        ],
        out_specs=pl.BlockSpec((1, SPAN, columns), lambda b: (0, b, 0)),
        compiler_params=params(),
        cost_estimate=pl.CostEstimate(
            flops=4 * rows * columns * SPAN, bytes_accessed=10 * rows * columns, transcendentals=0
        ),
        name="feedback",
    )(moment, masked, high, low)


def decode_kernel(replicas, groups, place_ref, mine_ref, theirs_ref, inverse_ref, high_ref, low_ref, *refs):
    parts, update_ref, whole_ref, dense_ref, sems = refs[:groups], *refs[groups:]
    width = parts[0].shape[1]

    def copies():
        for m in range(groups):
            at = pl.multiple_of((place_ref[0] ^ m) * width, width)
            yield pltpu.make_async_copy(parts[m], whole_ref.at[:, pl.ds(at, width)], sems.at[m])

    @pl.when(pl.program_id(0) == 0)
    def _():
        for copy in copies():
            copy.start()

    columns = mine_ref.shape[2]
    half = mine_ref.shape[1]
    second = place_ref[1] == 1
    mine = mine_ref[0].astype(jnp.float32) * (1.0 / replicas)
    theirs = theirs_ref[0].astype(jnp.float32) * (1.0 / replicas)
    first_half = jnp.where(second, theirs, mine)
    second_half = jnp.where(second, mine, theirs)
    for c in range(0, columns, LANES):
        source = [
            part[p : p + SUBLANES, c : c + LANES]
            for part in (first_half, second_half)
            for p in range(0, half, SUBLANES)
        ]
        for g in range(0, SPAN, SUBLANES):
            pick = inverse_ref[0, g : g + SUBLANES, c : c + LANES]
            inside, group = pick & (SUBLANES - 1), pick >> 3
            total = jnp.zeros((SUBLANES, LANES), jnp.float32)
            for s, rows in enumerate(source):
                total = jnp.where(group == s, jnp.take_along_axis(rows, inside, axis=0), total)
            dense_ref[g : g + SUBLANES, c : c + LANES] = total
    update_ref[...] = split_dot(high_ref[...], low_ref[...], dense_ref[...]).astype(jnp.bfloat16)

    @pl.when(pl.program_id(0) == pl.num_programs(0) - 1)
    def _():
        for copy in copies():
            copy.wait()


def decode(place, mine, theirs, inverse, high, low, parts, replicas):
    blocks, half, columns = mine.shape
    groups = len(parts)
    tokens, width = parts[0].shape
    whole = lambda b, place: (0, 0)
    by_block = lambda b, place: (b, 0, 0)
    return pl.pallas_call(
        functools.partial(decode_kernel, replicas, groups),
        out_shape=[
            jax.ShapeDtypeStruct((blocks * SPAN, columns), jnp.bfloat16),
            jax.ShapeDtypeStruct((tokens, groups * width), jnp.bfloat16),
        ],
        grid_spec=pltpu.PrefetchScalarGridSpec(
            num_scalar_prefetch=1,
            grid=(blocks,),
            in_specs=[
                pl.BlockSpec((1, half, columns), by_block),
                pl.BlockSpec((1, half, columns), by_block),
                pl.BlockSpec((1, SPAN, columns), by_block),
                pl.BlockSpec((SPAN, SPAN), whole),
                pl.BlockSpec((SPAN, SPAN), whole),
            ]
            + [pl.BlockSpec(memory_space=pl.ANY)] * groups,
            out_specs=[
                pl.BlockSpec((SPAN, columns), lambda b, place: (b, 0)),
                pl.BlockSpec(memory_space=pl.ANY),
            ],
            scratch_shapes=[
                pltpu.VMEM((SPAN, columns), jnp.float32),
                pltpu.SemaphoreType.DMA((groups,)),
            ],
        ),
        compiler_params=params(),
        cost_estimate=pl.CostEstimate(
            flops=6 * blocks * SPAN * SPAN * columns,
            bytes_accessed=6 * blocks * SPAN * columns + 4 * groups * tokens * width,
            transcendentals=0,
        ),
        name="decode",
    )(place, mine, theirs, inverse, high, low, *parts)


def swap(x, axis, mask):
    size = lax.axis_size(axis)
    return lax.ppermute(x, axis, [(s, s ^ mask) for s in range(size)])


def sum_over_chips(x):
    replicas = lax.axis_size("dp")
    stride = 2
    total = x
    while stride < replicas:
        sent = total.astype(jnp.bfloat16)
        parts = [sent] + [swap(sent, "dp", stride * m) for m in (1, 2, 3) if stride * m < replicas]
        parts = [part.astype(jnp.float32) for part in parts]
        total = parts[0] + parts[1] if len(parts) == 2 else (parts[0] + parts[1]) + (parts[2] + parts[3])
        stride *= 4
    return total.astype(jnp.bfloat16)


def on_device(activations, cotangent, weight, momentum, positions):
    groups, replicas = lax.axis_size("fsdp"), lax.axis_size("dp")
    rows = weight.shape[0]
    index = lax.axis_index("fsdp")
    place = jnp.stack([index, lax.axis_index("dp") % 2]).astype(jnp.int32)
    high, low = transform_table()

    cotangents = [cotangent] + [swap(cotangent, "fsdp", m) for m in range(1, groups)]
    inverse = inverse_index(positions)
    sent = [
        lax.dynamic_slice_in_dim(activations, (index ^ m) * rows, rows, 1) for m in range(1, groups)
    ]
    sent, cotangents = lax.optimization_barrier((sent, cotangents))
    inputs = [swap(sent[m - 1], "fsdp", m) for m in range(1, groups)]
    outer = input_gradients(cotangents, weight)
    inputs, inverse, _ = lax.optimization_barrier((inputs, inverse, outer))
    parts = [outer[0]] + [swap(outer[m], "fsdp", m) for m in range(1, groups)]

    moment, masked, mine, theirs = moments(
        place, activations, inputs, cotangents, momentum, positions, inverse, high, low
    )
    chip = mine.astype(jnp.float32) + swap(theirs, "dp", 1).astype(jnp.float32)
    moment, parts[1], parts[2] = lax.optimization_barrier((moment, parts[1], parts[2]))
    new_momentum = feedback(moment, masked, high.T, low.T)
    summed = sum_over_chips(chip)
    summed, new_momentum = lax.optimization_barrier((summed, new_momentum))
    update, grad_input = decode(
        place, summed, swap(summed, "dp", 1), inverse, high.T, low.T, parts, replicas
    )
    return grad_input, new_momentum, update


def solution(mesh):
    placed = (
        P(("dp", "fsdp"), None),
        P(("dp", "fsdp"), None),
        P("fsdp", None),
        P("dp", "fsdp", None),
        P("fsdp", None, None),
    )
    return jax.shard_map(
        on_device,
        mesh=mesh,
        in_specs=placed,
        out_specs=(P(("dp", "fsdp"), None), P("dp", "fsdp", None), P("fsdp", None)),
        check_vma=False,
    )
```

```python
import functools

import jax
import jax.numpy as jnp
import numpy as np
from jax import lax
from jax.experimental import pallas as pl
from jax.experimental.pallas import tpu as pltpu
from jax.sharding import PartitionSpec as P

SPAN = 256
MOMENTUM_DECAY = 0.999
LANES = 128
SUBLANES = 8
VMEM_LIMIT = 16 * 1024 * 1024


def transform_table():
    freq = np.arange(SPAN, dtype=np.float64)[:, None]
    place = np.arange(SPAN, dtype=np.float64)[None, :]
    scales = np.where(freq == 0.0, np.sqrt(1.0 / SPAN), np.sqrt(2.0 / SPAN))
    table = scales * np.cos(np.pi * (2.0 * place + 1.0) * freq / (2.0 * SPAN))
    high = table.astype(jnp.bfloat16)
    low = (table - high.astype(np.float64)).astype(jnp.bfloat16)
    return high, low


def two_terms(x):
    high = x.astype(jnp.bfloat16)
    return high, (x - high.astype(jnp.float32)).astype(jnp.bfloat16)


def dot(left, right):
    return jnp.dot(left, right, preferred_element_type=jnp.float32)


def split_dot(table_high, table_low, x):
    high, low = two_terms(x)
    return dot(table_high, high) + (dot(table_high, low) + dot(table_low, high))


def params(**more):
    return pltpu.CompilerParams(vmem_limit_bytes=VMEM_LIMIT, **more)


def inverse_index_kernel(positions_ref, inverse_ref):
    picks, columns = positions_ref.shape[1:]
    chunk = 64

    def one_chunk(at, carry):
        start = pl.multiple_of(at * chunk, chunk)
        for c in range(0, columns, LANES):
            where = positions_ref[0, :, c : c + LANES]
            level = lax.broadcasted_iota(jnp.int32, (chunk, LANES), 0) + start
            found = jnp.full((chunk, LANES), -1, jnp.int32)
            for i in range(picks):
                found = jnp.where(where[i : i + 1, :] == level, i, found)
            inverse_ref[0, pl.ds(start, chunk), c : c + LANES] = found
        return carry

    lax.fori_loop(0, SPAN // chunk, one_chunk, 0)


def inverse_index(positions):
    blocks, picks, columns = positions.shape
    return pl.pallas_call(
        inverse_index_kernel,
        out_shape=jax.ShapeDtypeStruct((blocks, SPAN, columns), jnp.int32),
        grid=(blocks,),
        in_specs=[pl.BlockSpec((1, picks, columns), lambda b: (b, 0, 0))],
        out_specs=pl.BlockSpec((1, SPAN, columns), lambda b: (b, 0, 0)),
        compiler_params=params(),
        cost_estimate=pl.CostEstimate(
            flops=2 * blocks * picks * SPAN * columns,
            bytes_accessed=4 * blocks * SPAN * columns,
            transcendentals=0,
        ),
        name="inverse_index",
    )(positions)


def cut_kernel(groups, place_ref, activations_ref, *refs):
    pieces, sems = refs[: groups - 1], refs[groups - 1]
    rows = pieces[0].shape[1]
    copies = []
    for m in range(1, groups):
        at = pl.multiple_of((place_ref[0] ^ m) * rows, rows)
        copies.append(
            pltpu.make_async_copy(
                activations_ref.at[:, pl.ds(at, rows)], pieces[m - 1], sems.at[m - 1]
            )
        )
    for copy in copies:
        copy.start()
    for copy in copies:
        copy.wait()


def cut(place, activations, groups):
    tokens, width = activations.shape
    rows = width // groups
    return pl.pallas_call(
        functools.partial(cut_kernel, groups),
        out_shape=[jax.ShapeDtypeStruct((tokens, rows), jnp.bfloat16)] * (groups - 1),
        in_specs=[
            pl.BlockSpec(memory_space=pltpu.SMEM),
            pl.BlockSpec(memory_space=pltpu.HBM),
        ],
        out_specs=[pl.BlockSpec(memory_space=pltpu.VMEM)] * (groups - 1),
        scratch_shapes=[pltpu.SemaphoreType.DMA((groups - 1,))],
        compiler_params=params(),
        cost_estimate=pl.CostEstimate(
            flops=0, bytes_accessed=4 * (groups - 1) * tokens * rows, transcendentals=0
        ),
        name="cut",
    )(place, activations)


def outer_kernel(groups, *refs):
    weight_ref = refs[groups]
    for s in range(groups):
        refs[groups + 1 + s][...] = lax.dot_general(
            refs[s][...],
            weight_ref[...],
            (((1,), (1,)), ((), ())),
            preferred_element_type=jnp.float32,
        ).astype(jnp.bfloat16)


def input_gradients(cotangents, weight):
    tokens, outputs = cotangents[0].shape
    rows = weight.shape[0]
    groups = len(cotangents)
    return pl.pallas_call(
        functools.partial(outer_kernel, groups),
        out_shape=[jax.ShapeDtypeStruct((tokens, rows), jnp.bfloat16)] * groups,
        compiler_params=params(),
        cost_estimate=pl.CostEstimate(
            flops=40 * groups * tokens * rows * outputs,
            bytes_accessed=2 * (groups * tokens * (rows + outputs) + rows * outputs),
            transcendentals=0,
        ),
        name="input_gradients",
    )(*cotangents, weight)


def moment_kernel(groups, place_ref, *refs):
    inputs, cotangents = refs[:groups], refs[groups : 2 * groups]
    momentum_ref, positions_ref, inverse_ref, high_ref, low_ref = refs[2 * groups : 2 * groups + 5]
    moment_ref, masked_ref, mine_ref, theirs_ref, coeffs_ref = refs[2 * groups + 5 :]
    picks, columns = positions_ref.shape[1:]
    gradient = None
    for s in range(groups):
        term = lax.dot_general(
            inputs[s][...],
            cotangents[s][...],
            (((0,), (0,)), ((), ())),
            preferred_element_type=jnp.float32,
        )
        gradient = term if gradient is None else gradient + term
    moment = MOMENTUM_DECAY * momentum_ref[0] + gradient
    moment_ref[...] = moment
    coeffs = split_dot(high_ref[...], low_ref[...], moment)
    coeffs_ref[...] = coeffs
    masked_ref[...] = jnp.where(inverse_ref[0] >= 0, coeffs, 0.0).astype(jnp.bfloat16)
    half = picks // 2
    parts = []
    for c in range(0, columns, LANES):
        found = []
        for p in range(0, picks, SUBLANES):
            where = positions_ref[0, p : p + SUBLANES, c : c + LANES]
            inside, group = where & (SUBLANES - 1), where // SUBLANES
            total = jnp.zeros((SUBLANES, LANES), jnp.float32)
            for g in range(SPAN // SUBLANES):
                rows = coeffs_ref[g * SUBLANES : (g + 1) * SUBLANES, c : c + LANES]
                total = jnp.where(
                    group == g, jnp.take_along_axis(rows, inside, axis=0), total
                )
            found.append(total)
        parts.append(jnp.concatenate(found, axis=0).astype(jnp.bfloat16))
    bands = jnp.concatenate(parts, axis=1)
    second = place_ref[1] == 1
    mine_ref[0] = jnp.where(second, bands[half:], bands[:half])
    theirs_ref[0] = jnp.where(second, bands[:half], bands[half:])


def moments(place, own_inputs, inputs, cotangents, momentum, positions, inverse, high, low):
    groups = len(cotangents)
    tokens, columns = cotangents[0].shape
    blocks, picks, _ = positions.shape
    whole = lambda b, place: (0, 0)
    half_shape = jax.ShapeDtypeStruct((blocks, picks // 2, columns), jnp.bfloat16)
    by_block = lambda b, place: (b, 0, 0)
    return pl.pallas_call(
        functools.partial(moment_kernel, groups),
        out_shape=[
            jax.ShapeDtypeStruct((blocks * SPAN, columns), jnp.float32),
            jax.ShapeDtypeStruct((blocks * SPAN, columns), jnp.bfloat16),
            half_shape,
            half_shape,
        ],
        grid_spec=pltpu.PrefetchScalarGridSpec(
            num_scalar_prefetch=1,
            grid=(blocks,),
            in_specs=[pl.BlockSpec((tokens, SPAN), lambda b, place: (0, place[0] * blocks + b))]
            + [pl.BlockSpec((tokens, SPAN), lambda b, place: (0, b))] * (groups - 1)
            + [pl.BlockSpec((tokens, columns), whole)] * groups
            + [
                pl.BlockSpec((1, SPAN, columns), lambda b, place: (0, b, 0)),
                pl.BlockSpec((1, picks, columns), by_block),
                pl.BlockSpec((1, SPAN, columns), by_block),
                pl.BlockSpec((SPAN, SPAN), whole),
                pl.BlockSpec((SPAN, SPAN), whole),
            ],
            out_specs=[
                pl.BlockSpec((SPAN, columns), lambda b, place: (b, 0)),
                pl.BlockSpec((SPAN, columns), lambda b, place: (b, 0)),
                pl.BlockSpec((1, picks // 2, columns), by_block),
                pl.BlockSpec((1, picks // 2, columns), by_block),
            ],
            scratch_shapes=[pltpu.VMEM((SPAN, columns), jnp.float32)],
        ),
        compiler_params=params(),
        cost_estimate=pl.CostEstimate(
            flops=2 * blocks * SPAN * columns * (groups * tokens + 3 * SPAN),
            bytes_accessed=blocks * SPAN * (groups * tokens * 2 + 14 * columns),
            transcendentals=0,
        ),
        name="moment",
    )(place, own_inputs, *inputs, *cotangents, momentum, positions, inverse, high, low)


def feedback_kernel(moment_ref, masked_ref, high_ref, low_ref, kept_ref):
    sent = dot(high_ref[...], masked_ref[...]) + dot(low_ref[...], masked_ref[...])
    kept_ref[0] = moment_ref[...] - sent


def feedback(moment, masked, high, low):
    rows, columns = moment.shape
    whole = lambda b: (0, 0)
    return pl.pallas_call(
        feedback_kernel,
        out_shape=jax.ShapeDtypeStruct((1, rows, columns), jnp.float32),
        grid=(rows // SPAN,),
        in_specs=[
            pl.BlockSpec((SPAN, columns), lambda b: (b, 0)),
            pl.BlockSpec((SPAN, columns), lambda b: (b, 0)),
            pl.BlockSpec((SPAN, SPAN), whole),
            pl.BlockSpec((SPAN, SPAN), whole),
        ],
        out_specs=pl.BlockSpec((1, SPAN, columns), lambda b: (0, b, 0)),
        compiler_params=params(),
        cost_estimate=pl.CostEstimate(
            flops=4 * rows * columns * SPAN, bytes_accessed=10 * rows * columns, transcendentals=0
        ),
        name="feedback",
    )(moment, masked, high, low)


def decode_kernel(replicas, groups, place_ref, mine_ref, theirs_ref, inverse_ref, high_ref, low_ref, *refs):
    parts, update_ref, whole_ref, dense_ref, sems = refs[:groups], *refs[groups:]
    width = parts[0].shape[1]

    def copies():
        for m in range(groups):
            at = pl.multiple_of((place_ref[0] ^ m) * width, width)
            yield pltpu.make_async_copy(parts[m], whole_ref.at[:, pl.ds(at, width)], sems.at[m])

    @pl.when(pl.program_id(0) == 0)
    def _():
        for copy in copies():
            copy.start()

    columns = mine_ref.shape[2]
    half = mine_ref.shape[1]
    second = place_ref[1] == 1
    mine = mine_ref[0].astype(jnp.float32) * (1.0 / replicas)
    theirs = theirs_ref[0].astype(jnp.float32) * (1.0 / replicas)
    first_half = jnp.where(second, theirs, mine)
    second_half = jnp.where(second, mine, theirs)
    for c in range(0, columns, LANES):
        source = [
            part[p : p + SUBLANES, c : c + LANES]
            for part in (first_half, second_half)
            for p in range(0, half, SUBLANES)
        ]
        for g in range(0, SPAN, SUBLANES):
            pick = inverse_ref[0, g : g + SUBLANES, c : c + LANES]
            inside, group = pick & (SUBLANES - 1), pick >> 3
            total = jnp.zeros((SUBLANES, LANES), jnp.float32)
            for s, rows in enumerate(source):
                total = jnp.where(group == s, jnp.take_along_axis(rows, inside, axis=0), total)
            dense_ref[g : g + SUBLANES, c : c + LANES] = total
    update_ref[...] = split_dot(high_ref[...], low_ref[...], dense_ref[...]).astype(jnp.bfloat16)

    @pl.when(pl.program_id(0) == pl.num_programs(0) - 1)
    def _():
        for copy in copies():
            copy.wait()


def decode(place, mine, theirs, inverse, high, low, parts, replicas):
    blocks, half, columns = mine.shape
    groups = len(parts)
    tokens, width = parts[0].shape
    whole = lambda b, place: (0, 0)
    by_block = lambda b, place: (b, 0, 0)
    return pl.pallas_call(
        functools.partial(decode_kernel, replicas, groups),
        out_shape=[
            jax.ShapeDtypeStruct((blocks * SPAN, columns), jnp.bfloat16),
            jax.ShapeDtypeStruct((tokens, groups * width), jnp.bfloat16),
        ],
        grid_spec=pltpu.PrefetchScalarGridSpec(
            num_scalar_prefetch=1,
            grid=(blocks,),
            in_specs=[
                pl.BlockSpec((1, half, columns), by_block),
                pl.BlockSpec((1, half, columns), by_block),
                pl.BlockSpec((1, SPAN, columns), by_block),
                pl.BlockSpec((SPAN, SPAN), whole),
                pl.BlockSpec((SPAN, SPAN), whole),
            ]
            + [pl.BlockSpec(memory_space=pl.ANY)] * groups,
            out_specs=[
                pl.BlockSpec((SPAN, columns), lambda b, place: (b, 0)),
                pl.BlockSpec(memory_space=pl.ANY),
            ],
            scratch_shapes=[
                pltpu.VMEM((SPAN, columns), jnp.float32),
                pltpu.SemaphoreType.DMA((groups,)),
            ],
        ),
        compiler_params=params(),
        cost_estimate=pl.CostEstimate(
            flops=6 * blocks * SPAN * SPAN * columns,
            bytes_accessed=6 * blocks * SPAN * columns + 4 * groups * tokens * width,
            transcendentals=0,
        ),
        name="decode",
    )(place, mine, theirs, inverse, high, low, *parts)


def swap(x, axis, mask):
    size = lax.axis_size(axis)
    return lax.ppermute(x, axis, [(s, s ^ mask) for s in range(size)])


def sum_over_chips(x, after):
    replicas = lax.axis_size("dp")
    stride = 2
    total = x
    while stride < replicas:
        sent = total.astype(jnp.bfloat16)
        masks = [stride * m for m in (1, 2, 3) if stride * m < replicas]
        late, after = lax.optimization_barrier((sent, after)) if stride == 2 else (sent, after)
        parts = [sent] + [swap(sent if m == masks[-1] else late, "dp", m) for m in masks]
        parts = [part.astype(jnp.float32) for part in parts]
        total = parts[0] + parts[1] if len(parts) == 2 else (parts[0] + parts[1]) + (parts[2] + parts[3])
        stride *= 4
    return total.astype(jnp.bfloat16), after


def on_device(activations, cotangent, weight, momentum, positions):
    groups, replicas = lax.axis_size("fsdp"), lax.axis_size("dp")
    rows = weight.shape[0]
    index = lax.axis_index("fsdp")
    place = jnp.stack([index, lax.axis_index("dp") % 2]).astype(jnp.int32)
    high, low = transform_table()

    cotangents = [cotangent] + [swap(cotangent, "fsdp", m) for m in range(1, groups)]
    inverse = inverse_index(positions)
    sent = cut(place, activations, groups)
    inputs = [swap(sent[m - 1], "fsdp", m) for m in range(1, groups)]
    outer = input_gradients(cotangents, weight)
    inputs, inverse, _ = lax.optimization_barrier((inputs, inverse, outer))
    parts = [outer[0]] + [swap(outer[m], "fsdp", m) for m in range(1, groups)]

    moment, masked, mine, theirs = moments(
        place, activations, inputs, cotangents, momentum, positions, inverse, high, low
    )
    chip = mine.astype(jnp.float32) + swap(theirs, "dp", 1).astype(jnp.float32)
    new_momentum = feedback(moment, masked, high.T, low.T)
    summed, parts[1:-1] = sum_over_chips(chip, parts[1:-1])
    summed, new_momentum = lax.optimization_barrier((summed, new_momentum))
    update, grad_input = decode(
        place, summed, swap(summed, "dp", 1), inverse, high.T, low.T, parts, replicas
    )
    return grad_input, new_momentum, update


def solution(mesh):
    placed = (
        P(("dp", "fsdp"), None),
        P(("dp", "fsdp"), None),
        P("fsdp", None),
        P("dp", "fsdp", None),
        P("fsdp", None, None),
    )
    return jax.shard_map(
        on_device,
        mesh=mesh,
        in_specs=placed,
        out_specs=(P(("dp", "fsdp"), None), P("dp", "fsdp", None), P("fsdp", None)),
        check_vma=False,
    )
```

```python
import functools

import jax
import jax.numpy as jnp
import numpy as np
from jax import lax
from jax.experimental import pallas as pl
from jax.experimental.pallas import tpu as pltpu
from jax.sharding import PartitionSpec as P

SPAN = 256
MOMENTUM_DECAY = 0.999
LANES = 128
SUBLANES = 8
VMEM_LIMIT = 16 * 1024 * 1024


def transform_table():
    freq = np.arange(SPAN, dtype=np.float64)[:, None]
    place = np.arange(SPAN, dtype=np.float64)[None, :]
    scales = np.where(freq == 0.0, np.sqrt(1.0 / SPAN), np.sqrt(2.0 / SPAN))
    table = scales * np.cos(np.pi * (2.0 * place + 1.0) * freq / (2.0 * SPAN))
    high = table.astype(jnp.bfloat16)
    low = (table - high.astype(np.float64)).astype(jnp.bfloat16)
    return high, low


def two_terms(x):
    high = x.astype(jnp.bfloat16)
    return high, (x - high.astype(jnp.float32)).astype(jnp.bfloat16)


def dot(left, right):
    return jnp.dot(left, right, preferred_element_type=jnp.float32)


def split_dot(table_high, table_low, x):
    high, low = two_terms(x)
    return dot(table_high, high) + (dot(table_high, low) + dot(table_low, high))


def params(**more):
    return pltpu.CompilerParams(vmem_limit_bytes=VMEM_LIMIT, **more)


def inverse_index_kernel(positions_ref, inverse_ref):
    blocks, picks, columns = positions_ref.shape
    chunk = 64
    per_block = SPAN // chunk

    def one_chunk(at, carry):
        b = at // per_block
        start = pl.multiple_of((at % per_block) * chunk, chunk)
        for c in range(0, columns, LANES):
            where = positions_ref[b, :, c : c + LANES]
            level = lax.broadcasted_iota(jnp.int32, (chunk, LANES), 0) + start
            found = jnp.full((chunk, LANES), -1, jnp.int32)
            for i in range(picks):
                found = jnp.where(where[i : i + 1, :] == level, i, found)
            inverse_ref[b, pl.ds(start, chunk), c : c + LANES] = found
        return carry

    lax.fori_loop(0, blocks * per_block, one_chunk, 0)


def inverse_index(positions):
    blocks, picks, columns = positions.shape
    return pl.pallas_call(
        inverse_index_kernel,
        out_shape=jax.ShapeDtypeStruct((blocks, SPAN, columns), jnp.int32),
        compiler_params=params(),
        cost_estimate=pl.CostEstimate(
            flops=2 * blocks * picks * SPAN * columns,
            bytes_accessed=4 * blocks * SPAN * columns,
            transcendentals=0,
        ),
        name="inverse_index",
    )(positions)


def cut_kernel(groups, place_ref, activations_ref, *refs):
    pieces, sems = refs[: groups - 1], refs[groups - 1]
    rows = pieces[0].shape[1]
    copies = []
    for m in range(1, groups):
        at = pl.multiple_of((place_ref[0] ^ m) * rows, rows)
        copies.append(
            pltpu.make_async_copy(
                activations_ref.at[:, pl.ds(at, rows)], pieces[m - 1], sems.at[m - 1]
            )
        )
    for copy in copies:
        copy.start()
    for copy in copies:
        copy.wait()


def cut(place, activations, groups):
    tokens, width = activations.shape
    rows = width // groups
    return pl.pallas_call(
        functools.partial(cut_kernel, groups),
        out_shape=[jax.ShapeDtypeStruct((tokens, rows), jnp.bfloat16)] * (groups - 1),
        in_specs=[
            pl.BlockSpec(memory_space=pltpu.SMEM),
            pl.BlockSpec(memory_space=pltpu.HBM),
        ],
        out_specs=[pl.BlockSpec(memory_space=pltpu.VMEM)] * (groups - 1),
        scratch_shapes=[pltpu.SemaphoreType.DMA((groups - 1,))],
        compiler_params=params(),
        cost_estimate=pl.CostEstimate(
            flops=0, bytes_accessed=4 * (groups - 1) * tokens * rows, transcendentals=0
        ),
        name="cut",
    )(place, activations)


def outer(cotangent, weight):
    return lax.dot_general(
        cotangent, weight, (((1,), (1,)), ((), ())), preferred_element_type=jnp.float32
    ).astype(jnp.bfloat16)


def outer_kernel(groups, *refs):
    weight_ref = refs[groups]
    for s in range(groups):
        refs[groups + 1 + s][...] = outer(refs[s][...], weight_ref[...])


def input_gradients(cotangents, weight):
    tokens, outputs = cotangents[0].shape
    rows = weight.shape[0]
    groups = len(cotangents)
    return pl.pallas_call(
        functools.partial(outer_kernel, groups),
        out_shape=[jax.ShapeDtypeStruct((tokens, rows), jnp.bfloat16)] * groups,
        in_specs=[pl.BlockSpec(memory_space=pltpu.VMEM)] * (groups + 1),
        out_specs=[pl.BlockSpec(memory_space=pltpu.VMEM)] * groups,
        compiler_params=params(),
        cost_estimate=pl.CostEstimate(
            flops=40 * groups * tokens * rows * outputs,
            bytes_accessed=2 * (groups * tokens * (rows + outputs) + rows * outputs),
            transcendentals=0,
        ),
        name="input_gradients",
    )(*cotangents, weight)


def across_tokens(left, right):
    return lax.dot_general(
        left, right, (((0,), (0,)), ((), ())), preferred_element_type=jnp.float32
    )


def early_kernel(groups, place_ref, *refs):
    inputs, cotangents = refs[:groups], refs[groups : 2 * groups]
    momentum_ref, high_ref, low_ref, moment_ref, coeffs_ref = refs[2 * groups :]
    blocks = moment_ref.shape[0] // SPAN
    for b in range(blocks):
        rows = slice(b * SPAN, (b + 1) * SPAN)
        own = pl.ds(pl.multiple_of((place_ref[0] * blocks + b) * SPAN, SPAN), SPAN)
        moment = MOMENTUM_DECAY * momentum_ref[0, rows, :]
        for s in range(groups):
            held = inputs[s][:, own if s == 0 else rows]
            moment = moment + across_tokens(held, cotangents[s][...])
        moment_ref[rows, :] = moment
        coeffs_ref[rows, :] = split_dot(high_ref[...], low_ref[...], moment)


def early_moments(place, activations, inputs, cotangents, momentum, high, low):
    groups = len(cotangents)
    tokens = cotangents[0].shape[0]
    _, rows, columns = momentum.shape
    return pl.pallas_call(
        functools.partial(early_kernel, groups),
        out_shape=[jax.ShapeDtypeStruct((rows, columns), jnp.float32)] * 2,
        in_specs=[pl.BlockSpec(memory_space=pltpu.SMEM)]
        + [pl.BlockSpec(memory_space=pltpu.VMEM)] * (2 * groups + 3),
        out_specs=[pl.BlockSpec(memory_space=pltpu.VMEM)] * 2,
        compiler_params=params(),
        cost_estimate=pl.CostEstimate(
            flops=2 * rows * columns * (groups * tokens + 3 * SPAN),
            bytes_accessed=rows * (groups * tokens * 2 + 12 * columns),
            transcendentals=0,
        ),
        name="early_moment",
    )(place, activations, *inputs, *cotangents, momentum, high, low)


def moment_kernel(groups, place_ref, *refs):
    inputs, cotangents = refs[:groups], refs[groups : 2 * groups - 1]
    (
        lower_ref,
        upper_ref,
        weight_ref,
        early_ref,
        early_coeffs_ref,
        positions_ref,
        high_ref,
        low_ref,
        moment_ref,
        coeffs_ref,
        mine_ref,
        theirs_ref,
        far_part_ref,
        far_ref,
    ) = refs[2 * groups - 1 :]
    token_half = lower_ref.shape[0]
    far_ref[:token_half, :] = lower_ref[...]
    far_ref[token_half:, :] = upper_ref[...]
    cotangents = (*cotangents, far_ref)
    far_part_ref[...] = outer(far_ref[...], weight_ref[...])
    blocks, picks, columns = positions_ref.shape
    half = picks // 2
    second = place_ref[1] == 1
    for b in range(blocks):
        rows = slice(b * SPAN, (b + 1) * SPAN)
        gradient = None
        for s in range(groups):
            term = across_tokens(inputs[s][:, rows], cotangents[s][...])
            gradient = term if gradient is None else gradient + term
        moment_ref[rows, :] = early_ref[rows, :] + gradient
        rounded = gradient.astype(jnp.bfloat16)
        coeffs_ref[rows, :] = early_coeffs_ref[rows, :] + (
            dot(high_ref[...], rounded) + dot(low_ref[...], rounded)
        )
        parts = []
        for c in range(0, columns, LANES):
            found = []
            for p in range(0, picks, SUBLANES):
                where = positions_ref[b, p : p + SUBLANES, c : c + LANES]
                inside, group = where & (SUBLANES - 1), where >> 3
                total = jnp.zeros((SUBLANES, LANES), jnp.float32)
                for g in range(SPAN // SUBLANES):
                    at = b * SPAN + g * SUBLANES
                    tile = coeffs_ref[at : at + SUBLANES, c : c + LANES]
                    total = jnp.where(
                        group == g, jnp.take_along_axis(tile, inside, axis=0), total
                    )
                found.append(total)
            parts.append(jnp.concatenate(found, axis=0).astype(jnp.bfloat16))
        bands = jnp.concatenate(parts, axis=1)
        mine_ref[b] = jnp.where(second, bands[half:], bands[:half])
        theirs_ref[b] = jnp.where(second, bands[:half], bands[half:])


def moments(place, inputs, cotangents, far_halves, weight, early, early_coeffs, positions, high, low):
    groups = len(inputs)
    tokens, rows = inputs[0].shape
    blocks, picks, columns = positions.shape
    half_shape = jax.ShapeDtypeStruct((blocks, picks // 2, columns), jnp.bfloat16)
    return pl.pallas_call(
        functools.partial(moment_kernel, groups),
        out_shape=[jax.ShapeDtypeStruct((rows, columns), jnp.float32)] * 2
        + [half_shape] * 2
        + [jax.ShapeDtypeStruct((tokens, rows), jnp.bfloat16)],
        in_specs=[pl.BlockSpec(memory_space=pltpu.SMEM)]
        + [pl.BlockSpec(memory_space=pltpu.VMEM)] * (2 * groups + 7),
        out_specs=[pl.BlockSpec(memory_space=pltpu.VMEM)] * 5,
        scratch_shapes=[pltpu.VMEM((tokens, columns), jnp.bfloat16)],
        compiler_params=params(),
        cost_estimate=pl.CostEstimate(
            flops=2 * blocks * SPAN * columns * (groups * tokens + 3 * SPAN),
            bytes_accessed=blocks * SPAN * (groups * tokens * 2 + 14 * columns),
            transcendentals=0,
        ),
        name="moment",
    )(
        place, *inputs, *cotangents, *far_halves, weight, early, early_coeffs, positions, high, low
    )


def feedback_kernel(moment_ref, coeffs_ref, inverse_ref, high_ref, low_ref, kept_ref, held_ref, sems):
    blocks = held_ref.shape[0]
    copies = []
    for b in range(blocks):
        rows = slice(b * SPAN, (b + 1) * SPAN)
        sent = jnp.where(inverse_ref[b] >= 0, coeffs_ref[rows, :], 0.0)
        held_ref[b] = moment_ref[rows, :] - split_dot(high_ref[...], low_ref[...], sent)
        copies.append(pltpu.make_async_copy(held_ref.at[b], kept_ref.at[0, rows, :], sems.at[b]))
        copies[-1].start()
    for copy in copies:
        copy.wait()


def feedback(moment, coeffs, inverse, high, low):
    rows, columns = moment.shape
    blocks = rows // SPAN
    return pl.pallas_call(
        feedback_kernel,
        out_shape=jax.ShapeDtypeStruct((1, rows, columns), jnp.float32),
        in_specs=[pl.BlockSpec(memory_space=pltpu.VMEM)] * 5,
        out_specs=pl.BlockSpec(memory_space=pltpu.HBM),
        scratch_shapes=[
            pltpu.VMEM((blocks, SPAN, columns), jnp.float32),
            pltpu.SemaphoreType.DMA((blocks,)),
        ],
        compiler_params=params(),
        cost_estimate=pl.CostEstimate(
            flops=4 * rows * columns * SPAN, bytes_accessed=10 * rows * columns, transcendentals=0
        ),
        name="feedback",
    )(moment, coeffs, inverse, high, low)


def decode_kernel(replicas, groups, place_ref, mine_ref, theirs_ref, inverse_ref, high_ref, low_ref, *refs):
    parts, update_ref, whole_ref, dense_ref, held_ref, sems, part_sems = (
        refs[:groups],
        *refs[groups:],
    )
    width = parts[0].shape[1]
    copies = []
    for m in range(groups):
        at = pl.multiple_of((place_ref[0] ^ m) * width, width)
        copies.append(
            pltpu.make_async_copy(parts[m], whole_ref.at[:, pl.ds(at, width)], part_sems.at[m])
        )
        copies[-1].start()

    blocks, half, columns = mine_ref.shape
    second = place_ref[1] == 1
    for b in range(blocks):
        mine = mine_ref[b].astype(jnp.float32)
        theirs = theirs_ref[b].astype(jnp.float32)
        first_half = jnp.where(second, theirs, mine)
        second_half = jnp.where(second, mine, theirs)
        for c in range(0, columns, LANES):
            source = [
                part[p : p + SUBLANES, c : c + LANES]
                for part in (first_half, second_half)
                for p in range(0, half, SUBLANES)
            ]
            for g in range(0, SPAN, SUBLANES):
                pick = inverse_ref[b, g : g + SUBLANES, c : c + LANES]
                inside, group = pick & (SUBLANES - 1), pick >> 3
                total = jnp.zeros((SUBLANES, LANES), jnp.float32)
                for s, tile in enumerate(source):
                    total = jnp.where(
                        group == s, jnp.take_along_axis(tile, inside, axis=0), total
                    )
                dense_ref[g : g + SUBLANES, c : c + LANES] = total
        dense = dense_ref[...].astype(jnp.bfloat16)
        update = (dot(high_ref[...], dense) + dot(low_ref[...], dense)) * (1.0 / replicas)
        held_ref[b] = update.astype(jnp.bfloat16)
        copies.append(
            pltpu.make_async_copy(
                held_ref.at[b], update_ref.at[b * SPAN : (b + 1) * SPAN, :], sems.at[b]
            )
        )
        copies[-1].start()
    for copy in copies:
        copy.wait()


def decode(place, mine, theirs, inverse, high, low, parts, replicas):
    blocks, half, columns = mine.shape
    groups = len(parts)
    tokens, width = parts[0].shape
    return pl.pallas_call(
        functools.partial(decode_kernel, replicas, groups),
        out_shape=[
            jax.ShapeDtypeStruct((blocks * SPAN, columns), jnp.bfloat16),
            jax.ShapeDtypeStruct((tokens, groups * width), jnp.bfloat16),
        ],
        in_specs=[pl.BlockSpec(memory_space=pltpu.SMEM)]
        + [pl.BlockSpec(memory_space=pltpu.VMEM)] * (5 + groups),
        out_specs=[pl.BlockSpec(memory_space=pltpu.HBM)] * 2,
        scratch_shapes=[
            pltpu.VMEM((SPAN, columns), jnp.float32),
            pltpu.VMEM((blocks, SPAN, columns), jnp.bfloat16),
            pltpu.SemaphoreType.DMA((blocks,)),
            pltpu.SemaphoreType.DMA((groups,)),
        ],
        compiler_params=params(),
        cost_estimate=pl.CostEstimate(
            flops=6 * blocks * SPAN * SPAN * columns,
            bytes_accessed=6 * blocks * SPAN * columns + 4 * groups * tokens * width,
            transcendentals=0,
        ),
        name="decode",
    )(place, mine, theirs, inverse, high, low, *parts)


def swap(x, axis, mask):
    size = lax.axis_size(axis)
    return lax.ppermute(x, axis, [(s, s ^ mask) for s in range(size)])


def sum_over_chips(x, after):
    replicas = lax.axis_size("dp")
    stride = 2
    total = x
    while stride < replicas:
        sent = total.astype(jnp.bfloat16)
        masks = [stride * m for m in (1, 2, 3) if stride * m < replicas]
        late, after = lax.optimization_barrier((sent, after)) if stride == 2 else (sent, after)
        parts = [sent] + [swap(late if m == masks[0] else sent, "dp", m) for m in masks]
        parts = [part.astype(jnp.float32) for part in parts]
        total = parts[0] + parts[1] if len(parts) == 2 else (parts[0] + parts[1]) + (parts[2] + parts[3])
        stride *= 4
    return total.astype(jnp.bfloat16), after


def far_cotangent(cotangents, groups):
    half = cotangents[0].shape[0] // 2
    if groups == 4:
        return swap(cotangents[2][:half], "fsdp", 1), swap(cotangents[1][half:], "fsdp", 2)
    far = swap(cotangents[0], "fsdp", groups - 1)
    return far[:half], far[half:]


def on_device(activations, cotangent, weight, momentum, positions):
    groups, replicas = lax.axis_size("fsdp"), lax.axis_size("dp")
    rows = weight.shape[0]
    index = lax.axis_index("fsdp")
    place = jnp.stack([index, lax.axis_index("dp") % 2]).astype(jnp.int32)
    high, low = transform_table()

    cotangents = [cotangent] + [swap(cotangent, "fsdp", m) for m in range(1, groups - 1)]
    far_halves = far_cotangent(cotangents, groups)
    inverse = inverse_index(positions)
    sent = cut(place, activations, groups)
    inputs = [swap(sent[m - 1], "fsdp", m) for m in range(1, groups)]
    near = input_gradients(cotangents, weight)
    late = groups - 2
    early, early_coeffs = early_moments(
        place, activations, inputs[: late - 1], cotangents[:late], momentum, high, low
    )
    inputs, inverse, early, _ = lax.optimization_barrier((inputs, inverse, early, near))
    parts = [near[0]] + [swap(near[m], "fsdp", m) for m in range(1, groups - 1)]

    moment, coeffs, mine, theirs, far = moments(
        place,
        inputs[late - 1 :],
        cotangents[late:],
        far_halves,
        weight,
        early,
        early_coeffs,
        positions,
        high,
        low,
    )
    parts.append(swap(far, "fsdp", groups - 1))
    chip = mine.astype(jnp.float32) + swap(theirs, "dp", 1).astype(jnp.float32)
    new_momentum = feedback(moment, coeffs, inverse, high.T, low.T)
    summed, parts[1:-1] = sum_over_chips(chip, parts[1:-1])
    summed, new_momentum = lax.optimization_barrier((summed, new_momentum))
    update, grad_input = decode(
        place, summed, swap(summed, "dp", 1), inverse, high.T, low.T, parts, replicas
    )
    return grad_input, new_momentum, update


def solution(mesh):
    placed = (
        P(("dp", "fsdp"), None),
        P(("dp", "fsdp"), None),
        P("fsdp", None),
        P("dp", "fsdp", None),
        P("fsdp", None, None),
    )
    return jax.shard_map(
        on_device,
        mesh=mesh,
        in_specs=placed,
        out_specs=(P(("dp", "fsdp"), None), P("dp", "fsdp", None), P("fsdp", None)),
        check_vma=False,
    )
```

```python
import functools

import jax
import jax.numpy as jnp
import numpy as np
from jax import lax
from jax.experimental import pallas as pl
from jax.experimental.pallas import tpu as pltpu
from jax.sharding import PartitionSpec as P

SPAN = 256
MOMENTUM_DECAY = 0.999
LANES = 128
SUBLANES = 8
VMEM_LIMIT = 16 * 1024 * 1024


def transform_table():
    freq = np.arange(SPAN, dtype=np.float64)[:, None]
    place = np.arange(SPAN, dtype=np.float64)[None, :]
    scales = np.where(freq == 0.0, np.sqrt(1.0 / SPAN), np.sqrt(2.0 / SPAN))
    table = scales * np.cos(np.pi * (2.0 * place + 1.0) * freq / (2.0 * SPAN))
    high = table.astype(jnp.bfloat16)
    low = (table - high.astype(np.float64)).astype(jnp.bfloat16)
    return high, low


def two_terms(x):
    high = x.astype(jnp.bfloat16)
    return high, (x - high.astype(jnp.float32)).astype(jnp.bfloat16)


def dot(left, right):
    return jnp.dot(left, right, preferred_element_type=jnp.float32)


def split_dot(table_high, table_low, x):
    high, low = two_terms(x)
    return dot(table_high, high) + (dot(table_high, low) + dot(table_low, high))


def params(**more):
    return pltpu.CompilerParams(vmem_limit_bytes=VMEM_LIMIT, **more)


def inverse_index_kernel(positions_ref, inverse_ref):
    blocks, picks, columns = positions_ref.shape
    chunk = 64
    per_block = SPAN // chunk

    def one_chunk(at, carry):
        b = at // per_block
        start = pl.multiple_of((at % per_block) * chunk, chunk)
        for c in range(0, columns, LANES):
            where = positions_ref[b, :, c : c + LANES]
            level = lax.broadcasted_iota(jnp.int32, (chunk, LANES), 0) + start
            found = jnp.full((chunk, LANES), -1, jnp.int32)
            for i in range(picks):
                found = jnp.where(where[i : i + 1, :] == level, i, found)
            inverse_ref[b, pl.ds(start, chunk), c : c + LANES] = found
        return carry

    lax.fori_loop(0, blocks * per_block, one_chunk, 0)


def inverse_index(positions):
    blocks, picks, columns = positions.shape
    return pl.pallas_call(
        inverse_index_kernel,
        out_shape=jax.ShapeDtypeStruct((blocks, SPAN, columns), jnp.int32),
        compiler_params=params(),
        cost_estimate=pl.CostEstimate(
            flops=2 * blocks * picks * SPAN * columns,
            bytes_accessed=4 * blocks * SPAN * columns,
            transcendentals=0,
        ),
        name="inverse_index",
    )(positions)


def cut_kernel(groups, place_ref, activations_ref, *refs):
    pieces, sems = refs[: groups - 1], refs[groups - 1]
    rows = pieces[0].shape[1]
    copies = []
    for m in range(1, groups):
        at = pl.multiple_of((place_ref[0] ^ m) * rows, rows)
        copies.append(
            pltpu.make_async_copy(
                activations_ref.at[:, pl.ds(at, rows)], pieces[m - 1], sems.at[m - 1]
            )
        )
    for copy in copies:
        copy.start()
    for copy in copies:
        copy.wait()


def cut(place, activations, groups):
    tokens, width = activations.shape
    rows = width // groups
    return pl.pallas_call(
        functools.partial(cut_kernel, groups),
        out_shape=[jax.ShapeDtypeStruct((tokens, rows), jnp.bfloat16)] * (groups - 1),
        in_specs=[
            pl.BlockSpec(memory_space=pltpu.SMEM),
            pl.BlockSpec(memory_space=pltpu.HBM),
        ],
        out_specs=[pl.BlockSpec(memory_space=pltpu.VMEM)] * (groups - 1),
        scratch_shapes=[pltpu.SemaphoreType.DMA((groups - 1,))],
        compiler_params=params(),
        cost_estimate=pl.CostEstimate(
            flops=0, bytes_accessed=4 * (groups - 1) * tokens * rows, transcendentals=0
        ),
        name="cut",
    )(place, activations)


def outer(cotangent, weight):
    return lax.dot_general(
        cotangent, weight, (((1,), (1,)), ((), ())), preferred_element_type=jnp.float32
    ).astype(jnp.bfloat16)


def outer_kernel(groups, *refs):
    weight_ref = refs[groups]
    for s in range(groups):
        refs[groups + 1 + s][...] = outer(refs[s][...], weight_ref[...])


def input_gradients(cotangents, weight):
    tokens, outputs = cotangents[0].shape
    rows = weight.shape[0]
    groups = len(cotangents)
    return pl.pallas_call(
        functools.partial(outer_kernel, groups),
        out_shape=[jax.ShapeDtypeStruct((tokens, rows), jnp.bfloat16)] * groups,
        in_specs=[pl.BlockSpec(memory_space=pltpu.VMEM)] * (groups + 1),
        out_specs=[pl.BlockSpec(memory_space=pltpu.VMEM)] * groups,
        compiler_params=params(),
        cost_estimate=pl.CostEstimate(
            flops=40 * groups * tokens * rows * outputs,
            bytes_accessed=2 * (groups * tokens * (rows + outputs) + rows * outputs),
            transcendentals=0,
        ),
        name="input_gradients",
    )(*cotangents, weight)


def across_tokens(left, right):
    return lax.dot_general(
        left, right, (((0,), (0,)), ((), ())), preferred_element_type=jnp.float32
    )


def early_kernel(groups, place_ref, *refs):
    inputs, cotangents = refs[:groups], refs[groups : 2 * groups]
    momentum_ref, high_ref, low_ref, moment_ref, coeffs_ref = refs[2 * groups :]
    blocks = moment_ref.shape[0] // SPAN
    for b in range(blocks):
        rows = slice(b * SPAN, (b + 1) * SPAN)
        own = pl.ds(pl.multiple_of((place_ref[0] * blocks + b) * SPAN, SPAN), SPAN)
        moment = MOMENTUM_DECAY * momentum_ref[0, rows, :]
        for s in range(groups):
            held = inputs[s][:, own if s == 0 else rows]
            moment = moment + across_tokens(held, cotangents[s][...])
        moment_ref[rows, :] = moment
        coeffs_ref[rows, :] = split_dot(high_ref[...], low_ref[...], moment)


def early_moments(place, activations, inputs, cotangents, momentum, high, low):
    groups = len(cotangents)
    tokens = cotangents[0].shape[0]
    _, rows, columns = momentum.shape
    return pl.pallas_call(
        functools.partial(early_kernel, groups),
        out_shape=[jax.ShapeDtypeStruct((rows, columns), jnp.float32)] * 2,
        in_specs=[pl.BlockSpec(memory_space=pltpu.SMEM)]
        + [pl.BlockSpec(memory_space=pltpu.VMEM)] * (2 * groups + 3),
        out_specs=[pl.BlockSpec(memory_space=pltpu.VMEM)] * 2,
        compiler_params=params(),
        cost_estimate=pl.CostEstimate(
            flops=2 * rows * columns * (groups * tokens + 3 * SPAN),
            bytes_accessed=rows * (groups * tokens * 2 + 12 * columns),
            transcendentals=0,
        ),
        name="early_moment",
    )(place, activations, *inputs, *cotangents, momentum, high, low)


def moment_kernel(groups, place_ref, *refs):
    inputs, cotangents = refs[:groups], refs[groups : 2 * groups - 1]
    (
        lower_ref,
        upper_ref,
        weight_ref,
        early_ref,
        early_coeffs_ref,
        positions_ref,
        high_ref,
        low_ref,
        moment_ref,
        coeffs_ref,
        mine_ref,
        theirs_ref,
        far_part_ref,
        far_ref,
    ) = refs[2 * groups - 1 :]
    token_half = lower_ref.shape[0]
    far_ref[:token_half, :] = lower_ref[...]
    far_ref[token_half:, :] = upper_ref[...]
    cotangents = (*cotangents, far_ref)
    far_part_ref[...] = outer(far_ref[...], weight_ref[...])
    blocks, picks, columns = positions_ref.shape
    half = picks // 2
    second = place_ref[1] == 1
    for b in range(blocks):
        rows = slice(b * SPAN, (b + 1) * SPAN)
        gradient = None
        for s in range(groups):
            term = across_tokens(inputs[s][:, rows], cotangents[s][...])
            gradient = term if gradient is None else gradient + term
        moment_ref[rows, :] = early_ref[rows, :] + gradient
        rounded = gradient.astype(jnp.bfloat16)
        coeffs_ref[rows, :] = early_coeffs_ref[rows, :] + (
            dot(high_ref[...], rounded) + dot(low_ref[...], rounded)
        )
        parts = []
        for c in range(0, columns, LANES):
            found = []
            for p in range(0, picks, SUBLANES):
                where = positions_ref[b, p : p + SUBLANES, c : c + LANES]
                inside, group = where & (SUBLANES - 1), where >> 3
                total = jnp.zeros((SUBLANES, LANES), jnp.float32)
                for g in range(SPAN // SUBLANES):
                    at = b * SPAN + g * SUBLANES
                    tile = coeffs_ref[at : at + SUBLANES, c : c + LANES]
                    total = jnp.where(
                        group == g, jnp.take_along_axis(tile, inside, axis=0), total
                    )
                found.append(total)
            parts.append(jnp.concatenate(found, axis=0).astype(jnp.bfloat16))
        bands = jnp.concatenate(parts, axis=1)
        mine_ref[b] = jnp.where(second, bands[half:], bands[:half])
        theirs_ref[b] = jnp.where(second, bands[:half], bands[half:])


def moments(place, inputs, cotangents, far_halves, weight, early, early_coeffs, positions, high, low):
    groups = len(inputs)
    tokens, rows = inputs[0].shape
    blocks, picks, columns = positions.shape
    half_shape = jax.ShapeDtypeStruct((blocks, picks // 2, columns), jnp.bfloat16)
    return pl.pallas_call(
        functools.partial(moment_kernel, groups),
        out_shape=[jax.ShapeDtypeStruct((rows, columns), jnp.float32)] * 2
        + [half_shape] * 2
        + [jax.ShapeDtypeStruct((tokens, rows), jnp.bfloat16)],
        in_specs=[pl.BlockSpec(memory_space=pltpu.SMEM)]
        + [pl.BlockSpec(memory_space=pltpu.VMEM)] * (2 * groups + 7),
        out_specs=[pl.BlockSpec(memory_space=pltpu.VMEM)] * 5,
        scratch_shapes=[pltpu.VMEM((tokens, columns), jnp.bfloat16)],
        compiler_params=params(),
        cost_estimate=pl.CostEstimate(
            flops=2 * blocks * SPAN * columns * (groups * tokens + 3 * SPAN),
            bytes_accessed=blocks * SPAN * (groups * tokens * 2 + 14 * columns),
            transcendentals=0,
        ),
        name="moment",
    )(
        place, *inputs, *cotangents, *far_halves, weight, early, early_coeffs, positions, high, low
    )


def start_copies(first, place_ref, parts, whole_ref, sems):
    width = parts[0].shape[1]
    copies = []
    for m, part in enumerate(parts):
        at = pl.multiple_of((place_ref[0] ^ (first + m)) * width, width)
        copies.append(pltpu.make_async_copy(part, whole_ref.at[:, pl.ds(at, width)], sems.at[m]))
        copies[-1].start()
    return copies


def feedback_kernel(groups, place_ref, moment_ref, coeffs_ref, inverse_ref, high_ref, low_ref, *refs):
    parts, kept_ref, whole_ref, held_ref, sems, part_sems = refs[:groups], *refs[groups:]
    copies = start_copies(0, place_ref, parts, whole_ref, part_sems)
    for b in range(held_ref.shape[0]):
        rows = slice(b * SPAN, (b + 1) * SPAN)
        sent = jnp.where(inverse_ref[b] >= 0, coeffs_ref[rows, :], 0.0)
        held_ref[b] = moment_ref[rows, :] - split_dot(high_ref[...], low_ref[...], sent)
        copies.append(pltpu.make_async_copy(held_ref.at[b], kept_ref.at[0, rows, :], sems.at[b]))
        copies[-1].start()
    for copy in copies:
        copy.wait()


def feedback(place, moment, coeffs, inverse, high, low, parts):
    rows, columns = moment.shape
    blocks = rows // SPAN
    groups = len(parts)
    tokens, width = parts[0].shape
    return pl.pallas_call(
        functools.partial(feedback_kernel, groups),
        out_shape=[
            jax.ShapeDtypeStruct((1, rows, columns), jnp.float32),
            jax.ShapeDtypeStruct((tokens, (groups + 1) * width), jnp.bfloat16),
        ],
        in_specs=[pl.BlockSpec(memory_space=pltpu.SMEM)]
        + [pl.BlockSpec(memory_space=pltpu.VMEM)] * (5 + groups),
        out_specs=[pl.BlockSpec(memory_space=pltpu.HBM)] * 2,
        scratch_shapes=[
            pltpu.VMEM((blocks, SPAN, columns), jnp.float32),
            pltpu.SemaphoreType.DMA((blocks,)),
            pltpu.SemaphoreType.DMA((groups,)),
        ],
        compiler_params=params(),
        cost_estimate=pl.CostEstimate(
            flops=6 * rows * columns * SPAN,
            bytes_accessed=16 * rows * columns + 4 * groups * tokens * width,
            transcendentals=0,
        ),
        name="feedback",
    )(place, moment, coeffs, inverse, high, low, *parts)


def put_in_place(bands_ref, inverse_ref, b, first, before):
    _, half, columns = bands_ref.shape
    bands = bands_ref[b].astype(jnp.float32)
    for c in range(0, columns, LANES):
        source = [bands[p : p + SUBLANES, c : c + LANES] for p in range(0, half, SUBLANES)]
        for g in range(0, SPAN, SUBLANES):
            at = (slice(g, g + SUBLANES), slice(c, c + LANES))
            pick = inverse_ref[b, *at]
            inside, group = pick & (SUBLANES - 1), (pick >> 3) - first
            total = before(at)
            for s, tile in enumerate(source):
                total = jnp.where(group == s, jnp.take_along_axis(tile, inside, axis=0), total)
            yield at, total


def place_kernel(place_ref, bands_ref, inverse_ref, dense_ref):
    blocks, half, _ = bands_ref.shape
    first = place_ref[1] * (half // SUBLANES)
    nothing = lambda at: jnp.zeros((SUBLANES, LANES), jnp.float32)
    for b in range(blocks):
        for at, tile in put_in_place(bands_ref, inverse_ref, b, first, nothing):
            dense_ref[b, *at] = tile


def place_own(place, bands, inverse):
    return pl.pallas_call(
        place_kernel,
        out_shape=jax.ShapeDtypeStruct(inverse.shape, jnp.float32),
        in_specs=[pl.BlockSpec(memory_space=pltpu.SMEM)]
        + [pl.BlockSpec(memory_space=pltpu.VMEM)] * 2,
        out_specs=pl.BlockSpec(memory_space=pltpu.VMEM),
        compiler_params=params(),
        cost_estimate=pl.CostEstimate(
            flops=8 * inverse.size, bytes_accessed=8 * inverse.size, transcendentals=0
        ),
        name="place_own",
    )(place, bands, inverse)


def decode_kernel(
    replicas,
    groups,
    place_ref,
    own_ref,
    theirs_ref,
    inverse_ref,
    high_ref,
    low_ref,
    part_ref,
    filled_ref,
    update_ref,
    whole_ref,
    dense_ref,
    held_ref,
    sems,
    part_sems,
):
    copies = start_copies(groups - 1, place_ref, [part_ref], whole_ref, part_sems)
    blocks, half, _ = theirs_ref.shape
    first = (1 - place_ref[1]) * (half // SUBLANES)
    for b in range(blocks):
        placed = lambda at: own_ref[b, *at]
        for at, tile in put_in_place(theirs_ref, inverse_ref, b, first, placed):
            dense_ref[b, *at] = tile
        dense = dense_ref[b].astype(jnp.bfloat16)
        update = (dot(high_ref[...], dense) + dot(low_ref[...], dense)) * (1.0 / replicas)
        held_ref[b] = update.astype(jnp.bfloat16)
        copies.append(
            pltpu.make_async_copy(
                held_ref.at[b], update_ref.at[b * SPAN : (b + 1) * SPAN, :], sems.at[b]
            )
        )
        copies[-1].start()
    for copy in copies:
        copy.wait()


def decode(place, own, theirs, inverse, high, low, part, filled, replicas):
    blocks, _, columns = theirs.shape
    tokens, width = part.shape
    groups = filled.shape[1] // width
    return pl.pallas_call(
        functools.partial(decode_kernel, replicas, groups),
        out_shape=[
            jax.ShapeDtypeStruct((blocks * SPAN, columns), jnp.bfloat16),
            jax.ShapeDtypeStruct(filled.shape, jnp.bfloat16),
        ],
        in_specs=[pl.BlockSpec(memory_space=pltpu.SMEM)]
        + [pl.BlockSpec(memory_space=pltpu.VMEM)] * 6
        + [pl.BlockSpec(memory_space=pltpu.HBM)],
        out_specs=[pl.BlockSpec(memory_space=pltpu.HBM)] * 2,
        scratch_shapes=[
            pltpu.VMEM((blocks, SPAN, columns), jnp.float32),
            pltpu.VMEM((blocks, SPAN, columns), jnp.bfloat16),
            pltpu.SemaphoreType.DMA((blocks,)),
            pltpu.SemaphoreType.DMA((1,)),
        ],
        input_output_aliases={7: 1},
        compiler_params=params(),
        cost_estimate=pl.CostEstimate(
            flops=6 * blocks * SPAN * SPAN * columns,
            bytes_accessed=6 * blocks * SPAN * columns + 4 * tokens * width,
            transcendentals=0,
        ),
        name="decode",
    )(place, own, theirs, inverse, high, low, part, filled)


def swap(x, axis, mask):
    size = lax.axis_size(axis)
    return lax.ppermute(x, axis, [(s, s ^ mask) for s in range(size)])


def sum_over_chips(x, after):
    replicas = lax.axis_size("dp")
    stride = 2
    total = x
    while stride < replicas:
        sent = total.astype(jnp.bfloat16)
        masks = [stride * m for m in (1, 2, 3) if stride * m < replicas]
        late, after = lax.optimization_barrier((sent, after)) if stride == 2 else (sent, after)
        parts = [sent] + [swap(late if m == masks[0] else sent, "dp", m) for m in masks]
        parts = [part.astype(jnp.float32) for part in parts]
        total = parts[0] + parts[1] if len(parts) == 2 else (parts[0] + parts[1]) + (parts[2] + parts[3])
        stride *= 4
    return total.astype(jnp.bfloat16), after


def far_cotangent(cotangents, groups):
    half = cotangents[0].shape[0] // 2
    if groups == 4:
        return swap(cotangents[2][:half], "fsdp", 1), swap(cotangents[1][half:], "fsdp", 2)
    far = swap(cotangents[0], "fsdp", groups - 1)
    return far[:half], far[half:]


def on_device(activations, cotangent, weight, momentum, positions):
    groups, replicas = lax.axis_size("fsdp"), lax.axis_size("dp")
    rows = weight.shape[0]
    index = lax.axis_index("fsdp")
    place = jnp.stack([index, lax.axis_index("dp") % 2]).astype(jnp.int32)
    high, low = transform_table()

    cotangents = [cotangent] + [swap(cotangent, "fsdp", m) for m in range(1, groups - 1)]
    far_halves = far_cotangent(cotangents, groups)
    inverse = inverse_index(positions)
    sent = cut(place, activations, groups)
    inputs = [swap(sent[m - 1], "fsdp", m) for m in range(1, groups)]
    near = input_gradients(cotangents, weight)
    late = groups - 2
    early, early_coeffs = early_moments(
        place, activations, inputs[: late - 1], cotangents[:late], momentum, high, low
    )
    inputs, inverse, early, _ = lax.optimization_barrier((inputs, inverse, early, near))
    parts = [near[0]] + [swap(near[m], "fsdp", m) for m in range(1, groups - 1)]

    moment, coeffs, mine, theirs, far = moments(
        place,
        inputs[late - 1 :],
        cotangents[late:],
        far_halves,
        weight,
        early,
        early_coeffs,
        positions,
        high,
        low,
    )
    parts.append(swap(far, "fsdp", groups - 1))
    chip = mine.astype(jnp.float32) + swap(theirs, "dp", 1).astype(jnp.float32)
    new_momentum, filled = feedback(place, moment, coeffs, inverse, high.T, low.T, parts[:-1])
    summed, parts[1:-1] = sum_over_chips(chip, parts[1:-1])
    summed, new_momentum = lax.optimization_barrier((summed, new_momentum))
    theirs = swap(summed, "dp", 1)
    own = place_own(place, summed, inverse)
    update, grad_input = decode(
        place, own, theirs, inverse, high.T, low.T, parts[-1], filled, replicas
    )
    return grad_input, new_momentum, update


def solution(mesh):
    placed = (
        P(("dp", "fsdp"), None),
        P(("dp", "fsdp"), None),
        P("fsdp", None),
        P("dp", "fsdp", None),
        P("fsdp", None, None),
    )
    return jax.shard_map(
        on_device,
        mesh=mesh,
        in_specs=placed,
        out_specs=(P(("dp", "fsdp"), None), P("dp", "fsdp", None), P("fsdp", None)),
        check_vma=False,
    )
```

```python
import functools

import jax
import jax.numpy as jnp
import numpy as np
from jax import lax
from jax.experimental import pallas as pl
from jax.experimental.pallas import tpu as pltpu
from jax.sharding import PartitionSpec as P

SPAN = 256
MOMENTUM_DECAY = 0.999
LANES = 128
SUBLANES = 8
VMEM_LIMIT = 16 * 1024 * 1024


def transform_table():
    freq = np.arange(SPAN, dtype=np.float64)[:, None]
    place = np.arange(SPAN, dtype=np.float64)[None, :]
    scales = np.where(freq == 0.0, np.sqrt(1.0 / SPAN), np.sqrt(2.0 / SPAN))
    table = scales * np.cos(np.pi * (2.0 * place + 1.0) * freq / (2.0 * SPAN))
    high = table.astype(jnp.bfloat16)
    low = (table - high.astype(np.float64)).astype(jnp.bfloat16)
    return high, low


def two_terms(x):
    high = x.astype(jnp.bfloat16)
    return high, (x - high.astype(jnp.float32)).astype(jnp.bfloat16)


def dot(left, right):
    return jnp.dot(left, right, preferred_element_type=jnp.float32)


def split_dot(table_high, table_low, x):
    high, low = two_terms(x)
    return dot(table_high, high) + (dot(table_high, low) + dot(table_low, high))


def params(**more):
    return pltpu.CompilerParams(vmem_limit_bytes=VMEM_LIMIT, **more)


def inverse_index_kernel(positions_ref, inverse_ref):
    blocks, picks, columns = positions_ref.shape
    chunk = 64
    per_block = SPAN // chunk

    def one_chunk(at, carry):
        b = at // per_block
        start = pl.multiple_of((at % per_block) * chunk, chunk)
        for c in range(0, columns, LANES):
            where = positions_ref[b, :, c : c + LANES]
            level = lax.broadcasted_iota(jnp.int32, (chunk, LANES), 0) + start
            found = jnp.full((chunk, LANES), -1, jnp.int32)
            for i in range(picks):
                found = jnp.where(where[i : i + 1, :] == level, i, found)
            inverse_ref[b, pl.ds(start, chunk), c : c + LANES] = found
        return carry

    lax.fori_loop(0, blocks * per_block, one_chunk, 0)


def inverse_index(positions):
    blocks, picks, columns = positions.shape
    return pl.pallas_call(
        inverse_index_kernel,
        out_shape=jax.ShapeDtypeStruct((blocks, SPAN, columns), jnp.int32),
        compiler_params=params(),
        cost_estimate=pl.CostEstimate(
            flops=2 * blocks * picks * SPAN * columns,
            bytes_accessed=4 * blocks * SPAN * columns,
            transcendentals=0,
        ),
        name="inverse_index",
    )(positions)


def cut_kernel(groups, place_ref, activations_ref, *refs):
    pieces, sems = refs[: groups - 1], refs[groups - 1]
    rows = pieces[0].shape[1]
    copies = []
    for m in range(1, groups):
        at = pl.multiple_of((place_ref[0] ^ m) * rows, rows)
        copies.append(
            pltpu.make_async_copy(
                activations_ref.at[:, pl.ds(at, rows)], pieces[m - 1], sems.at[m - 1]
            )
        )
    for copy in copies:
        copy.start()
    for copy in copies:
        copy.wait()


def cut(place, activations, groups):
    tokens, width = activations.shape
    rows = width // groups
    return pl.pallas_call(
        functools.partial(cut_kernel, groups),
        out_shape=[jax.ShapeDtypeStruct((tokens, rows), jnp.bfloat16)] * (groups - 1),
        in_specs=[
            pl.BlockSpec(memory_space=pltpu.SMEM),
            pl.BlockSpec(memory_space=pltpu.HBM),
        ],
        out_specs=[pl.BlockSpec(memory_space=pltpu.VMEM)] * (groups - 1),
        scratch_shapes=[pltpu.SemaphoreType.DMA((groups - 1,))],
        compiler_params=params(),
        cost_estimate=pl.CostEstimate(
            flops=0, bytes_accessed=4 * (groups - 1) * tokens * rows, transcendentals=0
        ),
        name="cut",
    )(place, activations)


def outer(cotangent, weight):
    return lax.dot_general(
        cotangent, weight, (((1,), (1,)), ((), ())), preferred_element_type=jnp.float32
    ).astype(jnp.bfloat16)


def outer_kernel(groups, *refs):
    weight_ref = refs[groups]
    for s in range(groups):
        refs[groups + 1 + s][...] = outer(refs[s][...], weight_ref[...])


def input_gradients(cotangents, weight):
    tokens, outputs = cotangents[0].shape
    rows = weight.shape[0]
    groups = len(cotangents)
    return pl.pallas_call(
        functools.partial(outer_kernel, groups),
        out_shape=[jax.ShapeDtypeStruct((tokens, rows), jnp.bfloat16)] * groups,
        in_specs=[pl.BlockSpec(memory_space=pltpu.VMEM)] * (groups + 1),
        out_specs=[pl.BlockSpec(memory_space=pltpu.VMEM)] * groups,
        compiler_params=params(),
        cost_estimate=pl.CostEstimate(
            flops=40 * groups * tokens * rows * outputs,
            bytes_accessed=2 * (groups * tokens * (rows + outputs) + rows * outputs),
            transcendentals=0,
        ),
        name="input_gradients",
    )(*cotangents, weight)


def across_tokens(left, right):
    return lax.dot_general(
        left, right, (((0,), (0,)), ((), ())), preferred_element_type=jnp.float32
    )


def early_kernel(groups, place_ref, *refs):
    inputs, cotangents = refs[:groups], refs[groups : 2 * groups]
    momentum_ref, high_ref, low_ref, moment_ref, coeffs_ref = refs[2 * groups :]
    blocks = moment_ref.shape[0] // SPAN
    for b in range(blocks):
        rows = slice(b * SPAN, (b + 1) * SPAN)
        own = pl.ds(pl.multiple_of((place_ref[0] * blocks + b) * SPAN, SPAN), SPAN)
        moment = MOMENTUM_DECAY * momentum_ref[0, rows, :]
        for s in range(groups):
            held = inputs[s][:, own if s == 0 else rows]
            moment = moment + across_tokens(held, cotangents[s][...])
        moment_ref[rows, :] = moment
        coeffs_ref[rows, :] = split_dot(high_ref[...], low_ref[...], moment)


def early_moments(place, activations, inputs, cotangents, momentum, high, low):
    groups = len(cotangents)
    tokens = cotangents[0].shape[0]
    _, rows, columns = momentum.shape
    return pl.pallas_call(
        functools.partial(early_kernel, groups),
        out_shape=[jax.ShapeDtypeStruct((rows, columns), jnp.float32)] * 2,
        in_specs=[pl.BlockSpec(memory_space=pltpu.SMEM)]
        + [pl.BlockSpec(memory_space=pltpu.VMEM)] * (2 * groups + 3),
        out_specs=[pl.BlockSpec(memory_space=pltpu.VMEM)] * 2,
        compiler_params=params(),
        cost_estimate=pl.CostEstimate(
            flops=2 * rows * columns * (groups * tokens + 3 * SPAN),
            bytes_accessed=rows * (groups * tokens * 2 + 12 * columns),
            transcendentals=0,
        ),
        name="early_moment",
    )(place, activations, *inputs, *cotangents, momentum, high, low)


def moment_kernel(groups, place_ref, *refs):
    inputs, cotangents = refs[:groups], refs[groups : 2 * groups - 1]
    (
        lower_ref,
        upper_ref,
        weight_ref,
        early_ref,
        early_coeffs_ref,
        positions_ref,
        high_ref,
        low_ref,
        moment_ref,
        coeffs_ref,
        mine_ref,
        theirs_ref,
        far_part_ref,
        far_ref,
    ) = refs[2 * groups - 1 :]
    token_half = lower_ref.shape[0]
    far_ref[:token_half, :] = lower_ref[...]
    far_ref[token_half:, :] = upper_ref[...]
    cotangents = (*cotangents, far_ref)
    far_part_ref[...] = outer(far_ref[...], weight_ref[...])
    blocks, picks, columns = positions_ref.shape
    half = picks // 2
    second = place_ref[1] == 1
    for b in range(blocks):
        rows = slice(b * SPAN, (b + 1) * SPAN)
        gradient = None
        for s in range(groups):
            term = across_tokens(inputs[s][:, rows], cotangents[s][...])
            gradient = term if gradient is None else gradient + term
        moment_ref[rows, :] = early_ref[rows, :] + gradient
        rounded = gradient.astype(jnp.bfloat16)
        coeffs_ref[rows, :] = early_coeffs_ref[rows, :] + (
            dot(high_ref[...], rounded) + dot(low_ref[...], rounded)
        )
        parts = []
        for c in range(0, columns, LANES):
            found = []
            for p in range(0, picks, SUBLANES):
                where = positions_ref[b, p : p + SUBLANES, c : c + LANES]
                inside, group = where & (SUBLANES - 1), where >> 3
                total = jnp.zeros((SUBLANES, LANES), jnp.float32)
                for g in range(SPAN // SUBLANES):
                    at = b * SPAN + g * SUBLANES
                    tile = coeffs_ref[at : at + SUBLANES, c : c + LANES]
                    total = jnp.where(
                        group == g, jnp.take_along_axis(tile, inside, axis=0), total
                    )
                found.append(total)
            parts.append(jnp.concatenate(found, axis=0).astype(jnp.bfloat16))
        bands = jnp.concatenate(parts, axis=1)
        mine_ref[b] = jnp.where(second, bands[half:], bands[:half])
        theirs_ref[b] = jnp.where(second, bands[:half], bands[half:])


def moments(place, inputs, cotangents, far_halves, weight, early, early_coeffs, positions, high, low):
    groups = len(inputs)
    tokens, rows = inputs[0].shape
    blocks, picks, columns = positions.shape
    half_shape = jax.ShapeDtypeStruct((blocks, picks // 2, columns), jnp.bfloat16)
    return pl.pallas_call(
        functools.partial(moment_kernel, groups),
        out_shape=[jax.ShapeDtypeStruct((rows, columns), jnp.float32)] * 2
        + [half_shape] * 2
        + [jax.ShapeDtypeStruct((tokens, rows), jnp.bfloat16)],
        in_specs=[pl.BlockSpec(memory_space=pltpu.SMEM)]
        + [pl.BlockSpec(memory_space=pltpu.VMEM)] * (2 * groups + 7),
        out_specs=[pl.BlockSpec(memory_space=pltpu.VMEM)] * 5,
        scratch_shapes=[pltpu.VMEM((tokens, columns), jnp.bfloat16)],
        compiler_params=params(),
        cost_estimate=pl.CostEstimate(
            flops=2 * blocks * SPAN * columns * (groups * tokens + 3 * SPAN),
            bytes_accessed=blocks * SPAN * (groups * tokens * 2 + 14 * columns),
            transcendentals=0,
        ),
        name="moment",
    )(
        place, *inputs, *cotangents, *far_halves, weight, early, early_coeffs, positions, high, low
    )


def start_copies(first, place_ref, parts, whole_ref, sems):
    width = parts[0].shape[1]
    copies = []
    for m, part in enumerate(parts):
        at = pl.multiple_of((place_ref[0] ^ (first + m)) * width, width)
        copies.append(pltpu.make_async_copy(part, whole_ref.at[:, pl.ds(at, width)], sems.at[m]))
        copies[-1].start()
    return copies


def feedback_kernel(groups, place_ref, moment_ref, coeffs_ref, inverse_ref, high_ref, low_ref, *refs):
    parts, kept_ref, whole_ref, held_ref, sems, part_sems = refs[:groups], *refs[groups:]
    copies = start_copies(0, place_ref, parts, whole_ref, part_sems)
    for b in range(held_ref.shape[0]):
        rows = slice(b * SPAN, (b + 1) * SPAN)
        sent = jnp.where(inverse_ref[b] >= 0, coeffs_ref[rows, :], 0.0)
        held_ref[b] = moment_ref[rows, :] - split_dot(high_ref[...], low_ref[...], sent)
        copies.append(pltpu.make_async_copy(held_ref.at[b], kept_ref.at[0, rows, :], sems.at[b]))
        copies[-1].start()
    for copy in copies:
        copy.wait()


def feedback(place, moment, coeffs, inverse, high, low, parts):
    rows, columns = moment.shape
    blocks = rows // SPAN
    groups = len(parts)
    tokens, width = parts[0].shape
    return pl.pallas_call(
        functools.partial(feedback_kernel, groups),
        out_shape=[
            jax.ShapeDtypeStruct((1, rows, columns), jnp.float32),
            jax.ShapeDtypeStruct((tokens, (groups + 1) * width), jnp.bfloat16),
        ],
        in_specs=[pl.BlockSpec(memory_space=pltpu.SMEM)]
        + [pl.BlockSpec(memory_space=pltpu.VMEM)] * (5 + groups),
        out_specs=[pl.BlockSpec(memory_space=pltpu.HBM)] * 2,
        scratch_shapes=[
            pltpu.VMEM((blocks, SPAN, columns), jnp.float32),
            pltpu.SemaphoreType.DMA((blocks,)),
            pltpu.SemaphoreType.DMA((groups,)),
        ],
        compiler_params=params(),
        cost_estimate=pl.CostEstimate(
            flops=6 * rows * columns * SPAN,
            bytes_accessed=16 * rows * columns + 4 * groups * tokens * width,
            transcendentals=0,
        ),
        name="feedback",
    )(place, moment, coeffs, inverse, high, low, *parts)


def put_in_place(bands_ref, inverse_ref, b, first, before):
    _, half, columns = bands_ref.shape
    bands = bands_ref[b].astype(jnp.float32)
    for c in range(0, columns, LANES):
        source = [bands[p : p + SUBLANES, c : c + LANES] for p in range(0, half, SUBLANES)]
        for g in range(0, SPAN, SUBLANES):
            at = (slice(g, g + SUBLANES), slice(c, c + LANES))
            pick = inverse_ref[b, *at]
            inside, group = pick & (SUBLANES - 1), (pick >> 3) - first
            total = before(at)
            for s, tile in enumerate(source):
                found = jnp.take_along_axis(tile, inside, axis=0, mode="promise_in_bounds")
                total = jnp.where(group == s, found, total)
            yield at, total


def place_kernel(place_ref, bands_ref, inverse_ref, dense_ref):
    blocks, half, _ = bands_ref.shape
    first = place_ref[1] * (half // SUBLANES)
    nothing = lambda at: jnp.zeros((SUBLANES, LANES), jnp.float32)
    for b in range(blocks):
        for at, tile in put_in_place(bands_ref, inverse_ref, b, first, nothing):
            dense_ref[b, *at] = tile


def place_own(place, bands, inverse):
    return pl.pallas_call(
        place_kernel,
        out_shape=jax.ShapeDtypeStruct(inverse.shape, jnp.float32),
        in_specs=[pl.BlockSpec(memory_space=pltpu.SMEM)]
        + [pl.BlockSpec(memory_space=pltpu.VMEM)] * 2,
        out_specs=pl.BlockSpec(memory_space=pltpu.VMEM),
        compiler_params=params(),
        cost_estimate=pl.CostEstimate(
            flops=8 * inverse.size, bytes_accessed=8 * inverse.size, transcendentals=0
        ),
        name="place_own",
    )(place, bands, inverse)


def decode_kernel(
    replicas,
    groups,
    place_ref,
    own_ref,
    theirs_ref,
    inverse_ref,
    high_ref,
    low_ref,
    part_ref,
    filled_ref,
    update_ref,
    whole_ref,
    dense_ref,
    held_ref,
    sems,
    part_sems,
):
    copies = start_copies(groups - 1, place_ref, [part_ref], whole_ref, part_sems)
    blocks, half, _ = theirs_ref.shape
    first = (1 - place_ref[1]) * (half // SUBLANES)

    def put(b):
        placed = lambda at: own_ref[b, *at]
        for at, tile in put_in_place(theirs_ref, inverse_ref, b, first, placed):
            dense_ref[b, *at] = tile

    put(0)
    for b in range(blocks):
        dense = dense_ref[b].astype(jnp.bfloat16)
        update = dot(high_ref[...], dense) + dot(low_ref[...], dense)
        if b + 1 < blocks:
            put(b + 1)
        held_ref[b] = (update * (1.0 / replicas)).astype(jnp.bfloat16)
        copies.append(
            pltpu.make_async_copy(
                held_ref.at[b], update_ref.at[b * SPAN : (b + 1) * SPAN, :], sems.at[b]
            )
        )
        copies[-1].start()
    for copy in copies:
        copy.wait()


def decode(place, own, theirs, inverse, high, low, part, filled, replicas):
    blocks, _, columns = theirs.shape
    tokens, width = part.shape
    groups = filled.shape[1] // width
    return pl.pallas_call(
        functools.partial(decode_kernel, replicas, groups),
        out_shape=[
            jax.ShapeDtypeStruct((blocks * SPAN, columns), jnp.bfloat16),
            jax.ShapeDtypeStruct(filled.shape, jnp.bfloat16),
        ],
        in_specs=[pl.BlockSpec(memory_space=pltpu.SMEM)]
        + [pl.BlockSpec(memory_space=pltpu.VMEM)] * 6
        + [pl.BlockSpec(memory_space=pltpu.HBM)],
        out_specs=[pl.BlockSpec(memory_space=pltpu.HBM)] * 2,
        scratch_shapes=[
            pltpu.VMEM((blocks, SPAN, columns), jnp.float32),
            pltpu.VMEM((blocks, SPAN, columns), jnp.bfloat16),
            pltpu.SemaphoreType.DMA((blocks,)),
            pltpu.SemaphoreType.DMA((1,)),
        ],
        input_output_aliases={7: 1},
        compiler_params=params(),
        cost_estimate=pl.CostEstimate(
            flops=6 * blocks * SPAN * SPAN * columns,
            bytes_accessed=6 * blocks * SPAN * columns + 4 * tokens * width,
            transcendentals=0,
        ),
        name="decode",
    )(place, own, theirs, inverse, high, low, part, filled)


def swap(x, axis, mask):
    size = lax.axis_size(axis)
    return lax.ppermute(x, axis, [(s, s ^ mask) for s in range(size)])


def sum_over_chips(x, after):
    replicas = lax.axis_size("dp")
    stride = 2
    total = x
    while stride < replicas:
        sent = total.astype(jnp.bfloat16)
        masks = [stride * m for m in (1, 2, 3) if stride * m < replicas]
        late, after = lax.optimization_barrier((sent, after)) if stride == 2 else (sent, after)
        parts = [sent] + [swap(late if m == masks[0] else sent, "dp", m) for m in masks]
        parts = [part.astype(jnp.float32) for part in parts]
        total = parts[0] + parts[1] if len(parts) == 2 else (parts[0] + parts[1]) + (parts[2] + parts[3])
        stride *= 4
    return total.astype(jnp.bfloat16), after


def far_cotangent(cotangents, groups):
    half = cotangents[0].shape[0] // 2
    if groups == 4:
        return swap(cotangents[2][:half], "fsdp", 1), swap(cotangents[1][half:], "fsdp", 2)
    far = swap(cotangents[0], "fsdp", groups - 1)
    return far[:half], far[half:]


def on_device(activations, cotangent, weight, momentum, positions):
    groups, replicas = lax.axis_size("fsdp"), lax.axis_size("dp")
    rows = weight.shape[0]
    index = lax.axis_index("fsdp")
    place = jnp.stack([index, lax.axis_index("dp") % 2]).astype(jnp.int32)
    high, low = transform_table()

    cotangents = [cotangent] + [swap(cotangent, "fsdp", m) for m in range(1, groups - 1)]
    far_halves = far_cotangent(cotangents, groups)
    inverse = inverse_index(positions)
    sent = cut(place, activations, groups)
    inputs = [swap(sent[m - 1], "fsdp", m) for m in range(1, groups)]
    near = input_gradients(cotangents, weight)
    late = groups - 2
    early, early_coeffs = early_moments(
        place, activations, inputs[: late - 1], cotangents[:late], momentum, high, low
    )
    inputs, inverse, early, _ = lax.optimization_barrier((inputs, inverse, early, near))
    parts = [near[0]] + [swap(near[m], "fsdp", m) for m in range(1, groups - 1)]

    moment, coeffs, mine, theirs, far = moments(
        place,
        inputs[late - 1 :],
        cotangents[late:],
        far_halves,
        weight,
        early,
        early_coeffs,
        positions,
        high,
        low,
    )
    parts.append(swap(far, "fsdp", groups - 1))
    chip = mine.astype(jnp.float32) + swap(theirs, "dp", 1).astype(jnp.float32)
    new_momentum, filled = feedback(place, moment, coeffs, inverse, high.T, low.T, parts[:-1])
    summed, parts[1:-1] = sum_over_chips(chip, parts[1:-1])
    summed, new_momentum = lax.optimization_barrier((summed, new_momentum))
    theirs = swap(summed, "dp", 1)
    own = place_own(place, summed, inverse)
    update, grad_input = decode(
        place, own, theirs, inverse, high.T, low.T, parts[-1], filled, replicas
    )
    return grad_input, new_momentum, update


def solution(mesh):
    placed = (
        P(("dp", "fsdp"), None),
        P(("dp", "fsdp"), None),
        P("fsdp", None),
        P("dp", "fsdp", None),
        P("fsdp", None, None),
    )
    return jax.shard_map(
        on_device,
        mesh=mesh,
        in_specs=placed,
        out_specs=(P(("dp", "fsdp"), None), P("dp", "fsdp", None), P("fsdp", None)),
        check_vma=False,
    )
```

```python
import functools

import jax
import jax.numpy as jnp
import numpy as np
from jax import lax
from jax.experimental import pallas as pl
from jax.experimental.pallas import tpu as pltpu
from jax.sharding import PartitionSpec as P

SPAN = 256
MOMENTUM_DECAY = 0.999
LANES = 128
SUBLANES = 8
VMEM_LIMIT = 16 * 1024 * 1024


def transform_table():
    freq = np.arange(SPAN, dtype=np.float64)[:, None]
    place = np.arange(SPAN, dtype=np.float64)[None, :]
    scales = np.where(freq == 0.0, np.sqrt(1.0 / SPAN), np.sqrt(2.0 / SPAN))
    table = scales * np.cos(np.pi * (2.0 * place + 1.0) * freq / (2.0 * SPAN))
    high = table.astype(jnp.bfloat16)
    low = (table - high.astype(np.float64)).astype(jnp.bfloat16)
    return high, low


def two_terms(x):
    high = x.astype(jnp.bfloat16)
    return high, (x - high.astype(jnp.float32)).astype(jnp.bfloat16)


def dot(left, right):
    return jnp.dot(left, right, preferred_element_type=jnp.float32)


def split_dot(table_high, table_low, x):
    high, low = two_terms(x)
    return dot(table_high, high) + (dot(table_high, low) + dot(table_low, high))


def params(**more):
    return pltpu.CompilerParams(vmem_limit_bytes=VMEM_LIMIT, **more)


def inverse_index_kernel(positions_ref, inverse_ref):
    blocks, picks, columns = positions_ref.shape
    chunk = 64
    per_block = SPAN // chunk

    def one_chunk(at, carry):
        b = at // per_block
        start = pl.multiple_of((at % per_block) * chunk, chunk)
        for c in range(0, columns, LANES):
            where = positions_ref[b, :, c : c + LANES]
            level = lax.broadcasted_iota(jnp.int32, (chunk, LANES), 0) + start
            found = jnp.full((chunk, LANES), -1, jnp.int32)
            for i in range(picks):
                found = jnp.where(where[i : i + 1, :] == level, i, found)
            inverse_ref[b, pl.ds(start, chunk), c : c + LANES] = found
        return carry

    lax.fori_loop(0, blocks * per_block, one_chunk, 0)


def inverse_index(positions):
    blocks, picks, columns = positions.shape
    return pl.pallas_call(
        inverse_index_kernel,
        out_shape=jax.ShapeDtypeStruct((blocks, SPAN, columns), jnp.int32),
        compiler_params=params(),
        cost_estimate=pl.CostEstimate(
            flops=2 * blocks * picks * SPAN * columns,
            bytes_accessed=4 * blocks * SPAN * columns,
            transcendentals=0,
        ),
        name="inverse_index",
    )(positions)


def cut_kernel(groups, place_ref, activations_ref, *refs):
    pieces, sems = refs[: groups - 1], refs[groups - 1]
    rows = pieces[0].shape[1]
    copies = []
    for m in range(1, groups):
        at = pl.multiple_of((place_ref[0] ^ m) * rows, rows)
        copies.append(
            pltpu.make_async_copy(
                activations_ref.at[:, pl.ds(at, rows)], pieces[m - 1], sems.at[m - 1]
            )
        )
    for copy in copies:
        copy.start()
    for copy in copies:
        copy.wait()


def cut(place, activations, groups):
    tokens, width = activations.shape
    rows = width // groups
    return pl.pallas_call(
        functools.partial(cut_kernel, groups),
        out_shape=[jax.ShapeDtypeStruct((tokens, rows), jnp.bfloat16)] * (groups - 1),
        in_specs=[
            pl.BlockSpec(memory_space=pltpu.SMEM),
            pl.BlockSpec(memory_space=pltpu.HBM),
        ],
        out_specs=[pl.BlockSpec(memory_space=pltpu.VMEM)] * (groups - 1),
        scratch_shapes=[pltpu.SemaphoreType.DMA((groups - 1,))],
        compiler_params=params(),
        cost_estimate=pl.CostEstimate(
            flops=0, bytes_accessed=4 * (groups - 1) * tokens * rows, transcendentals=0
        ),
        name="cut",
    )(place, activations)


def outer(cotangent, weight):
    return lax.dot_general(
        cotangent, weight, (((1,), (1,)), ((), ())), preferred_element_type=jnp.float32
    ).astype(jnp.bfloat16)


def outer_kernel(groups, *refs):
    weight_ref = refs[groups]
    for s in range(groups):
        refs[groups + 1 + s][...] = outer(refs[s][...], weight_ref[...])


def input_gradients(cotangents, weight):
    tokens, outputs = cotangents[0].shape
    rows = weight.shape[0]
    groups = len(cotangents)
    return pl.pallas_call(
        functools.partial(outer_kernel, groups),
        out_shape=[jax.ShapeDtypeStruct((tokens, rows), jnp.bfloat16)] * groups,
        in_specs=[pl.BlockSpec(memory_space=pltpu.VMEM)] * (groups + 1),
        out_specs=[pl.BlockSpec(memory_space=pltpu.VMEM)] * groups,
        compiler_params=params(),
        cost_estimate=pl.CostEstimate(
            flops=40 * groups * tokens * rows * outputs,
            bytes_accessed=2 * (groups * tokens * (rows + outputs) + rows * outputs),
            transcendentals=0,
        ),
        name="input_gradients",
    )(*cotangents, weight)


def across_tokens(left, right):
    return lax.dot_general(
        left, right, (((0,), (0,)), ((), ())), preferred_element_type=jnp.float32
    )


def early_kernel(groups, place_ref, *refs):
    inputs, cotangents = refs[:groups], refs[groups : 2 * groups]
    momentum_ref, high_ref, low_ref, moment_ref, coeffs_ref = refs[2 * groups :]
    blocks = moment_ref.shape[0] // SPAN
    for b in range(blocks):
        rows = slice(b * SPAN, (b + 1) * SPAN)
        own = pl.ds(pl.multiple_of((place_ref[0] * blocks + b) * SPAN, SPAN), SPAN)
        moment = MOMENTUM_DECAY * momentum_ref[0, rows, :]
        for s in range(groups):
            held = inputs[s][:, own if s == 0 else rows]
            moment = moment + across_tokens(held, cotangents[s][...])
        moment_ref[rows, :] = moment
        coeffs_ref[rows, :] = split_dot(high_ref[...], low_ref[...], moment)


def early_moments(place, activations, inputs, cotangents, momentum, high, low):
    groups = len(cotangents)
    tokens = cotangents[0].shape[0]
    _, rows, columns = momentum.shape
    return pl.pallas_call(
        functools.partial(early_kernel, groups),
        out_shape=[jax.ShapeDtypeStruct((rows, columns), jnp.float32)] * 2,
        in_specs=[pl.BlockSpec(memory_space=pltpu.SMEM)]
        + [pl.BlockSpec(memory_space=pltpu.VMEM)] * (2 * groups + 3),
        out_specs=[pl.BlockSpec(memory_space=pltpu.VMEM)] * 2,
        compiler_params=params(),
        cost_estimate=pl.CostEstimate(
            flops=2 * rows * columns * (groups * tokens + 3 * SPAN),
            bytes_accessed=rows * (groups * tokens * 2 + 12 * columns),
            transcendentals=0,
        ),
        name="early_moment",
    )(place, activations, *inputs, *cotangents, momentum, high, low)


def moment_kernel(groups, place_ref, *refs):
    inputs, cotangents = refs[:groups], refs[groups : 2 * groups - 1]
    (
        lower_ref,
        upper_ref,
        weight_ref,
        early_ref,
        early_coeffs_ref,
        positions_ref,
        high_ref,
        low_ref,
        moment_ref,
        coeffs_ref,
        mine_ref,
        theirs_ref,
        far_part_ref,
        far_ref,
    ) = refs[2 * groups - 1 :]
    token_half = lower_ref.shape[0]
    far_ref[:token_half, :] = lower_ref[...]
    far_ref[token_half:, :] = upper_ref[...]
    cotangents = (*cotangents, far_ref)
    far_part_ref[...] = outer(far_ref[...], weight_ref[...])
    blocks, picks, columns = positions_ref.shape
    half = picks // 2
    second = place_ref[1] == 1
    for b in range(blocks):
        rows = slice(b * SPAN, (b + 1) * SPAN)
        gradient = None
        for s in range(groups):
            term = across_tokens(inputs[s][:, rows], cotangents[s][...])
            gradient = term if gradient is None else gradient + term
        moment_ref[rows, :] = early_ref[rows, :] + gradient
        rounded = gradient.astype(jnp.bfloat16)
        coeffs_ref[rows, :] = early_coeffs_ref[rows, :] + (
            dot(high_ref[...], rounded) + dot(low_ref[...], rounded)
        )
        parts = []
        for c in range(0, columns, LANES):
            found = []
            for p in range(0, picks, SUBLANES):
                where = positions_ref[b, p : p + SUBLANES, c : c + LANES]
                inside, group = where & (SUBLANES - 1), where >> 3
                total = jnp.zeros((SUBLANES, LANES), jnp.float32)
                for g in range(SPAN // SUBLANES):
                    at = b * SPAN + g * SUBLANES
                    tile = coeffs_ref[at : at + SUBLANES, c : c + LANES]
                    total = jnp.where(
                        group == g, jnp.take_along_axis(tile, inside, axis=0), total
                    )
                found.append(total)
            parts.append(jnp.concatenate(found, axis=0).astype(jnp.bfloat16))
        bands = jnp.concatenate(parts, axis=1)
        mine_ref[b] = jnp.where(second, bands[half:], bands[:half])
        theirs_ref[b] = jnp.where(second, bands[:half], bands[half:])


def moments(place, inputs, cotangents, far_halves, weight, early, early_coeffs, positions, high, low):
    groups = len(inputs)
    tokens, rows = inputs[0].shape
    blocks, picks, columns = positions.shape
    half_shape = jax.ShapeDtypeStruct((blocks, picks // 2, columns), jnp.bfloat16)
    return pl.pallas_call(
        functools.partial(moment_kernel, groups),
        out_shape=[jax.ShapeDtypeStruct((rows, columns), jnp.float32)] * 2
        + [half_shape] * 2
        + [jax.ShapeDtypeStruct((tokens, rows), jnp.bfloat16)],
        in_specs=[pl.BlockSpec(memory_space=pltpu.SMEM)]
        + [pl.BlockSpec(memory_space=pltpu.VMEM)] * (2 * groups + 7),
        out_specs=[pl.BlockSpec(memory_space=pltpu.VMEM)] * 5,
        scratch_shapes=[pltpu.VMEM((tokens, columns), jnp.bfloat16)],
        compiler_params=params(),
        cost_estimate=pl.CostEstimate(
            flops=2 * blocks * SPAN * columns * (groups * tokens + 3 * SPAN),
            bytes_accessed=blocks * SPAN * (groups * tokens * 2 + 14 * columns),
            transcendentals=0,
        ),
        name="moment",
    )(
        place, *inputs, *cotangents, *far_halves, weight, early, early_coeffs, positions, high, low
    )


def start_copies(first, place_ref, parts, whole_ref, sems):
    width = parts[0].shape[1]
    copies = []
    for m, part in enumerate(parts):
        at = pl.multiple_of((place_ref[0] ^ (first + m)) * width, width)
        copies.append(pltpu.make_async_copy(part, whole_ref.at[:, pl.ds(at, width)], sems.at[m]))
        copies[-1].start()
    return copies


def feedback_kernel(groups, place_ref, moment_ref, coeffs_ref, inverse_ref, high_ref, low_ref, *refs):
    parts, kept_ref, whole_ref, held_ref, sems, part_sems = refs[:groups], *refs[groups:]
    copies = start_copies(0, place_ref, parts, whole_ref, part_sems)
    for b in range(held_ref.shape[0]):
        rows = slice(b * SPAN, (b + 1) * SPAN)
        sent = jnp.where(inverse_ref[b] >= 0, coeffs_ref[rows, :], 0.0)
        held_ref[b] = moment_ref[rows, :] - split_dot(high_ref[...], low_ref[...], sent)
        copies.append(pltpu.make_async_copy(held_ref.at[b], kept_ref.at[0, rows, :], sems.at[b]))
        copies[-1].start()
    for copy in copies:
        copy.wait()


def feedback(place, moment, coeffs, inverse, high, low, parts):
    rows, columns = moment.shape
    blocks = rows // SPAN
    groups = len(parts)
    tokens, width = parts[0].shape
    return pl.pallas_call(
        functools.partial(feedback_kernel, groups),
        out_shape=[
            jax.ShapeDtypeStruct((1, rows, columns), jnp.float32),
            jax.ShapeDtypeStruct((tokens, (groups + 1) * width), jnp.bfloat16),
        ],
        in_specs=[pl.BlockSpec(memory_space=pltpu.SMEM)]
        + [pl.BlockSpec(memory_space=pltpu.VMEM)] * (5 + groups),
        out_specs=[pl.BlockSpec(memory_space=pltpu.HBM)] * 2,
        scratch_shapes=[
            pltpu.VMEM((blocks, SPAN, columns), jnp.float32),
            pltpu.SemaphoreType.DMA((blocks,)),
            pltpu.SemaphoreType.DMA((groups,)),
        ],
        compiler_params=params(),
        cost_estimate=pl.CostEstimate(
            flops=6 * rows * columns * SPAN,
            bytes_accessed=16 * rows * columns + 4 * groups * tokens * width,
            transcendentals=0,
        ),
        name="feedback",
    )(place, moment, coeffs, inverse, high, low, *parts)


def put_in_place(bands_ref, inverse_ref, b, first, before):
    _, half, columns = bands_ref.shape
    bands = bands_ref[b].astype(jnp.float32)
    for c in range(0, columns, LANES):
        source = [bands[p : p + SUBLANES, c : c + LANES] for p in range(0, half, SUBLANES)]
        for g in range(0, SPAN, SUBLANES):
            at = (slice(g, g + SUBLANES), slice(c, c + LANES))
            pick = inverse_ref[b, *at]
            inside, group = pick & (SUBLANES - 1), (pick >> 3) - first
            total = before(at)
            for s, tile in enumerate(source):
                total = jnp.where(group == s, jnp.take_along_axis(tile, inside, axis=0), total)
            yield at, total


def place_kernel(place_ref, bands_ref, inverse_ref, dense_ref):
    blocks, half, _ = bands_ref.shape
    first = place_ref[1] * (half // SUBLANES)
    nothing = lambda at: jnp.zeros((SUBLANES, LANES), jnp.float32)
    for b in range(blocks):
        for at, tile in put_in_place(bands_ref, inverse_ref, b, first, nothing):
            dense_ref[b, *at] = tile


def place_own(place, bands, inverse):
    return pl.pallas_call(
        place_kernel,
        out_shape=jax.ShapeDtypeStruct(inverse.shape, jnp.float32),
        in_specs=[pl.BlockSpec(memory_space=pltpu.SMEM)]
        + [pl.BlockSpec(memory_space=pltpu.VMEM)] * 2,
        out_specs=pl.BlockSpec(memory_space=pltpu.VMEM),
        compiler_params=params(),
        cost_estimate=pl.CostEstimate(
            flops=8 * inverse.size, bytes_accessed=8 * inverse.size, transcendentals=0
        ),
        name="place_own",
    )(place, bands, inverse)


def decode_kernel(
    replicas,
    groups,
    place_ref,
    own_ref,
    theirs_ref,
    inverse_ref,
    high_ref,
    low_ref,
    part_ref,
    filled_ref,
    update_ref,
    whole_ref,
    dense_ref,
    held_ref,
    sems,
    part_sems,
):
    copies = start_copies(groups - 1, place_ref, [part_ref], whole_ref, part_sems)
    blocks, half, _ = theirs_ref.shape
    first = (1 - place_ref[1]) * (half // SUBLANES)
    for b in range(blocks):
        placed = lambda at: own_ref[b, *at]
        for at, tile in put_in_place(theirs_ref, inverse_ref, b, first, placed):
            dense_ref[b, *at] = tile
        dense = dense_ref[b].astype(jnp.bfloat16)
        update = (dot(high_ref[...], dense) + dot(low_ref[...], dense)) * (1.0 / replicas)
        held_ref[b] = update.astype(jnp.bfloat16)
        copies.append(
            pltpu.make_async_copy(
                held_ref.at[b], update_ref.at[b * SPAN : (b + 1) * SPAN, :], sems.at[b]
            )
        )
        copies[-1].start()
    for copy in copies:
        copy.wait()


def decode(place, own, theirs, inverse, high, low, part, filled, replicas):
    blocks, _, columns = theirs.shape
    tokens, width = part.shape
    groups = filled.shape[1] // width
    return pl.pallas_call(
        functools.partial(decode_kernel, replicas, groups),
        out_shape=[
            jax.ShapeDtypeStruct((blocks * SPAN, columns), jnp.bfloat16),
            jax.ShapeDtypeStruct(filled.shape, jnp.bfloat16),
        ],
        in_specs=[pl.BlockSpec(memory_space=pltpu.SMEM)]
        + [pl.BlockSpec(memory_space=pltpu.VMEM)] * 6
        + [pl.BlockSpec(memory_space=pltpu.HBM)],
        out_specs=[pl.BlockSpec(memory_space=pltpu.HBM)] * 2,
        scratch_shapes=[
            pltpu.VMEM((blocks, SPAN, columns), jnp.float32),
            pltpu.VMEM((blocks, SPAN, columns), jnp.bfloat16),
            pltpu.SemaphoreType.DMA((blocks,)),
            pltpu.SemaphoreType.DMA((1,)),
        ],
        input_output_aliases={7: 1},
        compiler_params=params(),
        cost_estimate=pl.CostEstimate(
            flops=6 * blocks * SPAN * SPAN * columns,
            bytes_accessed=6 * blocks * SPAN * columns + 4 * tokens * width,
            transcendentals=0,
        ),
        name="decode",
    )(place, own, theirs, inverse, high, low, part, filled)


def swap(x, axis, mask):
    size = lax.axis_size(axis)
    return lax.ppermute(x, axis, [(s, s ^ mask) for s in range(size)])


def sum_over_chips(x, after):
    replicas = lax.axis_size("dp")
    stride = 2
    total = x
    while stride < replicas:
        sent = total.astype(jnp.bfloat16)
        masks = [stride * m for m in (1, 2, 3) if stride * m < replicas]
        late, after = lax.optimization_barrier((sent, after)) if stride == 2 else (sent, after)
        parts = [sent] + [swap(late if m == masks[0] else sent, "dp", m) for m in masks]
        parts = [part.astype(jnp.float32) for part in parts]
        total = parts[0] + parts[1] if len(parts) == 2 else (parts[0] + parts[1]) + (parts[2] + parts[3])
        stride *= 4
    return total.astype(jnp.bfloat16), after


def far_cotangent(cotangents, groups):
    half = cotangents[0].shape[0] // 2
    if groups == 4:
        return swap(cotangents[2][:half], "fsdp", 1), swap(cotangents[1][half:], "fsdp", 2)
    far = swap(cotangents[0], "fsdp", groups - 1)
    return far[:half], far[half:]


def on_device(activations, cotangent, weight, momentum, positions):
    groups, replicas = lax.axis_size("fsdp"), lax.axis_size("dp")
    rows = weight.shape[0]
    index = lax.axis_index("fsdp")
    place = jnp.stack([index, lax.axis_index("dp") % 2]).astype(jnp.int32)
    high, low = transform_table()

    cotangents = [cotangent] + [swap(cotangent, "fsdp", m) for m in range(1, groups - 1)]
    far_halves = far_cotangent(cotangents, groups)
    inverse = inverse_index(positions)
    sent = cut(place, activations, groups)
    inputs = [swap(sent[m - 1], "fsdp", m) for m in range(1, groups)]
    near = input_gradients(cotangents, weight)
    late = groups - 2
    early, early_coeffs = early_moments(
        place, activations, inputs[: late - 1], cotangents[:late], momentum, high, low
    )
    inputs, inverse, early, _ = lax.optimization_barrier((inputs, inverse, early, near))
    near = list(near)
    near[1], early = lax.optimization_barrier((near[1], early))
    parts = [near[0]] + [swap(near[m], "fsdp", m) for m in range(1, groups - 1)]

    moment, coeffs, mine, theirs, far = moments(
        place,
        inputs[late - 1 :],
        cotangents[late:],
        far_halves,
        weight,
        early,
        early_coeffs,
        positions,
        high,
        low,
    )
    parts.append(swap(far, "fsdp", groups - 1))
    chip = mine.astype(jnp.float32) + swap(theirs, "dp", 1).astype(jnp.float32)
    new_momentum, filled = feedback(place, moment, coeffs, inverse, high.T, low.T, parts[:-1])
    summed, parts[1:-1] = sum_over_chips(chip, parts[1:-1])
    summed, new_momentum = lax.optimization_barrier((summed, new_momentum))
    theirs = swap(summed, "dp", 1)
    own = place_own(place, summed, inverse)
    update, grad_input = decode(
        place, own, theirs, inverse, high.T, low.T, parts[-1], filled, replicas
    )
    return grad_input, new_momentum, update


def solution(mesh):
    placed = (
        P(("dp", "fsdp"), None),
        P(("dp", "fsdp"), None),
        P("fsdp", None),
        P("dp", "fsdp", None),
        P("fsdp", None, None),
    )
    return jax.shard_map(
        on_device,
        mesh=mesh,
        in_specs=placed,
        out_specs=(P(("dp", "fsdp"), None), P("dp", "fsdp", None), P("fsdp", None)),
        check_vma=False,
    )
```
